256 devices in a mesh: row: 32 (over z, x), col: 8 (over y, core).
Axes of the slice: x: 4, y: 4, z: 8, core: 2. Of those that a mesh axis runs over, the one named last changes fastest.
Arguments:
- normed_input: bfloat16 [2048, 16384], P('col', 'row'), may hold values from -6 to 6
- attended: bfloat16 [2048, 16384], P('col', 'row'), may hold values from -6 to 6
- qkv_grad: bfloat16 [2048, 18432], P('row', 'col'), may hold values from -0.13183594 to 0.13183594
- proj_grad: bfloat16 [2048, 16384], P('row', 'col'), may hold values from -0.13183594 to 0.13183594
Outputs:
- qkv_weight_grad: bfloat16 [16384, 18432], P('row', 'col')
- out_weight_grad: bfloat16 [16384, 16384], P('row', 'col')
The draws below stay inside these ranges and needn't reach their ends.
All inputs are finite; a program needn't handle non-finite values.
Results may differ from the reference program's by a relative error of at most 0.001.
Values may be sent and summed in bfloat16 or wider, within the bound.
No kernel may reach another device: no remote copies, remote signals or barrier semaphores. Data moves between devices by JAX's collectives and lax.ppermute only.
A program may use at most 128 MiB of HBM per device.

```python
import jax
import jax.numpy as jnp

D = 16384
QKV = 18432
ATT = 16384
TOKENS = 2048


def block_scale(rng, shape, pieces, smallest, high):
    def one(dim, parts):
        heights = jax.random.uniform(jax.random.fold_in(jax.random.fold_in(rng, 6), dim), (parts,), jnp.float32, smallest / len(pieces), high / len(pieces))
        return jnp.repeat(jnp.exp(heights), shape[dim] // parts).reshape((-1,) + (1,) * (len(shape) - dim - 1))

    loudness = one(*pieces[0])
    for cut in pieces[1:]:
        loudness = loudness * one(*cut)
    return loudness


def gaussian(stream_key, dims, deviation, limit, cuts=(), kind=jnp.bfloat16):
    array = jax.random.normal(stream_key, dims, jnp.float32) * deviation
    if len(cuts) > 0:
        array = block_scale(stream_key, dims, cuts, -0.22, 0.18) * array
    return jnp.clip(array, min=-limit, max=limit).astype(kind)


def setup_inputs(seed: int = 0) -> dict:
    seeds = jax.random.split(jax.random.key(seed), 5)
    normed_input = gaussian(seeds[0], (TOKENS, D), 1.0, 6.0, ((0, 8), (1, 32)))
    attended = gaussian(seeds[1], (TOKENS, ATT), 1.0, 6.0, ((0, 8), (1, 32)))
    qkv_grad = gaussian(seeds[2], (TOKENS, QKV), (TOKENS ** -0.5), 0.13183594, ((0, 32), (1, 8)))
    proj_grad = gaussian(seeds[3], (TOKENS, D), (TOKENS ** -0.5), 0.13183594, ((0, 32), (1, 8)))
    return dict(normed_input=normed_input, attended=attended, qkv_grad=qkv_grad, proj_grad=proj_grad)


def reference(normed_input, attended, qkv_grad, proj_grad):
    qkv_weight_grad = jnp.dot(normed_input.T, qkv_grad, preferred_element_type=jnp.float32).astype(jnp.bfloat16)
    out_weight_grad = jnp.dot(attended.T, proj_grad, preferred_element_type=jnp.float32).astype(jnp.bfloat16)
    return qkv_weight_grad, out_weight_grad
```

```python
import jax
import jax.numpy as jnp
from jax import lax
from jax.sharding import PartitionSpec as P

Z, X = 8, 4


def hop(value, dz, dx):
    pairs = [
        (z * X + x, ((z + dz) % Z) * X + (x + dx) % X) for z in range(Z) for x in range(X)
    ]
    return lax.ppermute(value, "row", pairs)


def ring(value, size, step):
    up = lambda v: hop(v, *step)
    down = lambda v: hop(v, -step[0], -step[1])
    blocks = {0: value}
    below = above = value
    for distance in range(1, size // 2):
        below, above = up(below), down(above)
        blocks[-distance], blocks[distance] = below, above
    half = value.shape[0] // 2
    blocks[size // 2] = jnp.concatenate([up(below[:half]), down(above[half:])])
    return blocks


Z_ORDER = (0, -1, 1, -2, 2, -3, 3, 4)
X_ORDER = (0, -1, 1, 2)


def contract(left, right):
    return lax.dot_general(
        left, right, (((0,), (0,)), ((), ())), preferred_element_type=jnp.float32
    )


def body(normed_input, attended, qkv_grad, proj_grad):
    place = lax.axis_index("row")
    z, x = place // X, place % X
    features = normed_input.shape[1]
    both = lax.all_gather(
        jnp.concatenate([normed_input, attended], axis=1), "col", axis=0, tiled=True
    )
    tokens = both.shape[0]
    both = both.reshape(Z, X, tokens // (Z * X), 2 * features)
    both = lax.dynamic_slice_in_dim(jnp.concatenate([both, both], 0), z, Z, 0)
    both = lax.dynamic_slice_in_dim(jnp.concatenate([both, both], 1), x, X, 1)

    def tokens_at(dz, dx, op):
        return both[dz % Z, dx % X, :, op * features : (op + 1) * features]

    near = ring(proj_grad, X, (0, 1))
    far = ring(jnp.concatenate([near[d] for d in X_ORDER]), Z, (1, 0))
    tall = ring(qkv_grad, Z, (1, 0))
    wide = ring(jnp.concatenate([tall[d] for d in Z_ORDER]), X, (0, 1))

    qkv = 0
    for dx in X_ORDER:
        left = jnp.concatenate([tokens_at(dz, dx, 0) for dz in Z_ORDER])
        qkv = qkv + contract(left, wide[dx])
    out = 0
    for dz in Z_ORDER:
        left = jnp.concatenate([tokens_at(dz, dx, 1) for dx in X_ORDER])
        out = out + contract(left, far[dz])
    return qkv.astype(jnp.bfloat16), out.astype(jnp.bfloat16)


def solution(mesh):
    placed = (P("col", "row"), P("col", "row"), P("row", "col"), P("row", "col"))
    return jax.shard_map(
        body,
        mesh=mesh,
        in_specs=placed,
        out_specs=(P("row", "col"), P("row", "col")),
        check_vma=False,
    )
```

```python
import functools

import jax
import jax.numpy as jnp
from jax import lax
from jax.experimental import pallas as pl
from jax.experimental.pallas import tpu as pltpu
from jax.sharding import PartitionSpec as P

Z, X, Y, C = 8, 4, 4, 2
BLOCK = 64
FEATURES = 512
TILE = 256
SPLIT = 256

X_ORDER = (0, -1, 1, 2)
NEAR, FAR = (0, -1, 1), (-2, 2, -3, 3, 4)


def hop(value, dz, dx):
    pairs = [
        (z * X + x, ((z + dz) % Z) * X + (x + dx) % X) for z in range(Z) for x in range(X)
    ]
    return lax.ppermute(value, "row", pairs)


def hop_y(value, dy, swap=0):
    pairs = [(y * C + c, ((y + dy) % Y) * C + (c ^ swap)) for y in range(Y) for c in range(C)]
    return lax.ppermute(value, "col", pairs)


def halves(value):
    half = value.shape[0] // 2
    return value[:half], value[half:]


def kernel(rows, sizes, added, ops, tiles, prefix, place_ref, mine_ref, other_ref, *refs):
    grads, refs = refs[: len(sizes)], refs[len(sizes) :]
    if added:
        total_ref, *refs = refs
    if prefix:
        prefix_ref, *refs = refs
    *outs, left, right, turned, sems = refs
    tile = pl.program_id(0)

    @pl.when(tile == 0)
    def _():
        z, x, y, core = (place_ref[i] for i in range(4))
        features = pl.ds(ops[0] * FEATURES, len(ops) * FEATURES)
        at = 0
        for i, (dz, dx, start, size) in enumerate(rows):
            group = lax.rem(z + (dz + Z), Z)
            away = lax.rem(group // C + Y - y, Y)
            slot = jnp.where(away == 0, 0, jnp.where(away == Y - 1, 1, jnp.where(away == 1, 2, 3)))
            row = slot * (X * BLOCK) + lax.rem(x + (dx + X), X) * BLOCK + start
            source = pl.ds(pl.multiple_of(row, 32), size)
            target = left.at[pl.ds(at, size)]
            swapped = lax.rem(group, C) != core

            @pl.when(swapped)
            def _():
                pltpu.make_async_copy(other_ref.at[source, features], target, sems.at[i]).start()

            @pl.when(jnp.logical_not(swapped))
            def _():
                pltpu.make_async_copy(mine_ref.at[source, features], target, sems.at[i]).start()

            at += size
        at = 0
        for i, (_, _, _, size) in enumerate(rows):
            span = left.at[pl.ds(at, size)]
            pltpu.make_async_copy(span, span, sems.at[i]).wait()
            at += size
        for i in range(len(ops)):
            turned[i] = left[:, i * FEATURES : (i + 1) * FEATURES].T

    def work(op, out_ref):
        at = 0
        for grad, size in zip(grads, sizes):
            right[pl.ds(at, size)] = grad[...]
            at += size
        part = jnp.dot(turned[op], right[...], preferred_element_type=jnp.float32)
        if added:
            part += total_ref[...]
        out_ref[...] = part.astype(out_ref.dtype)

    if prefix:
        pl.when(tile < prefix)(lambda: outs[0].__setitem__(..., prefix_ref[...]))
        pl.when(tile >= prefix)(lambda: work(0, outs[0]))
    elif len(ops) == 1:
        work(0, outs[0])
    else:
        pl.when(tile < tiles)(lambda: work(0, outs[0]))
        pl.when(tile >= tiles)(lambda: work(1, outs[-1]))


def contract(place, operand, ops, blocks, total=None, prefix=None, split=None, dtype=jnp.float32):
    grads = [array for array, _ in blocks]
    rows = [row for _, some in blocks for row in some]
    sizes = [array.shape[0] for array in grads]
    depth, width = sum(sizes), grads[0].shape[1]
    assert depth == sum(row[3] for row in rows)
    ahead = 0 if prefix is None else prefix.shape[1] // TILE
    tiles = ahead + width // TILE
    cut = tiles if split is None else split // TILE
    anywhere = pl.BlockSpec(memory_space=pl.ANY)
    here = lambda height: pl.BlockSpec((height, TILE), lambda t: (0, jnp.maximum(t - ahead, 0)))
    if dtype == jnp.float32 or len(ops) == 1:
        widths, specs = [tiles * TILE], [pl.BlockSpec((FEATURES, TILE), lambda t: (0, t))]
    else:
        widths = [cut * TILE, (tiles - cut) * TILE]
        specs = [
            pl.BlockSpec((FEATURES, TILE), lambda t: (0, jnp.minimum(t, cut - 1))),
            pl.BlockSpec((FEATURES, TILE), lambda t: (0, jnp.maximum(t - cut, 0))),
        ]
    extra, extra_specs = [], []
    if total is not None:
        extra, extra_specs = [total], [here(FEATURES)]
    if prefix is not None:
        extra.append(prefix)
        extra_specs.append(
            pl.BlockSpec((FEATURES, TILE), lambda t: (0, jnp.minimum(t, ahead - 1)))
        )
    results = pl.pallas_call(
        functools.partial(kernel, rows, sizes, total is not None, ops, cut, ahead),
        grid=(tiles,),
        out_shape=[jax.ShapeDtypeStruct((FEATURES, w), dtype) for w in widths],
        in_specs=[pl.BlockSpec(memory_space=pltpu.SMEM), anywhere, anywhere]
        + [here(size) for size in sizes]
        + extra_specs,
        out_specs=specs,
        scratch_shapes=[
            pltpu.VMEM((depth, len(ops) * FEATURES), jnp.bfloat16),
            pltpu.VMEM((depth, TILE), jnp.bfloat16),
            pltpu.VMEM((len(ops), FEATURES, depth), jnp.bfloat16),
            pltpu.SemaphoreType.DMA((len(rows),)),
        ],
        compiler_params=pltpu.CompilerParams(vmem_limit_bytes=24 << 20),
        cost_estimate=pl.CostEstimate(
            flops=2 * FEATURES * depth * width,
            bytes_accessed=2 * depth * (width + FEATURES) + 4 * FEATURES * width,
            transcendentals=0,
        ),
    )(place, *operand, *grads, *extra)
    return results if len(results) > 1 else results[0]


def whole(dzs, dx):
    return [(dz, dx, 0, BLOCK) for dz in dzs]


def parts(rows):
    half, first, second = sum(row[3] for row in rows) // 2, [], []
    for dz, dx, start, size in rows:
        here = min(size, half)
        if here:
            first.append((dz, dx, start, here))
        if here < size:
            second.append((dz, dx, start + here, size - here))
        half -= here
    return first, second


def body(normed_input, attended, qkv_grad, proj_grad):
    row, col = lax.axis_index("row"), lax.axis_index("col")
    place = jnp.stack([row // X, row % X, col // C, col % C])

    tall = jnp.concatenate([qkv_grad, proj_grad[:, :SPLIT]], axis=1)
    wide = proj_grad[:, SPLIT:]

    below, above = hop(tall, 1, 0), hop(tall, -1, 0)
    left, right = hop(wide, 0, 1), hop(wide, 0, -1)
    near = jnp.concatenate([tall, below, above])
    far = []
    for distance in (2, 3):
        below, above = hop(below, 1, 0), hop(above, -1, 0)
        far += [below, above]
    far += [hop(halves(below)[0], 1, 0), hop(halves(above)[1], -1, 0)]
    left_half, right_half = hop(halves(left)[0], 0, 1), hop(halves(right)[1], 0, -1)
    wide = jnp.concatenate([wide, left, right, left_half, right_half])

    mine = jnp.concatenate([normed_input, attended], axis=1)
    down, up = hop_y(mine, 1), hop_y(mine, -1)
    mine = jnp.concatenate(
        [mine, down, up, hop_y(halves(down)[0], 1), hop_y(halves(up)[1], -1)]
    )
    operand = (mine, hop_y(mine, 0, 1))

    near_left, near_right = hop(near, 0, 1), hop(near, 0, -1)
    near_rows = {dx: whole(NEAR, dx) for dx in X_ORDER}
    far, wide, below, above = lax.optimization_barrier((far, wide, below, above))
    far = jnp.concatenate(far)
    far_rows = {dx: whole(FAR, dx) for dx in X_ORDER}
    far_left, far_right = hop(far, 0, 1), hop(far, 0, -1)
    near_split, far_split = parts(near_rows[2]), parts(far_rows[2])
    tall_first = [
        (near, near_rows[0]),
        (near_left, near_rows[-1]),
        (near_right, near_rows[1]),
        (hop(halves(near_left)[0], 0, 1), near_split[0]),
        (hop(halves(near_right)[1], 0, -1), near_split[1]),
        (far, far_rows[0]),
    ]
    tall_second = [(far_left, far_rows[-1]), (far_right, far_rows[1])]
    width = qkv_grad.shape[1]
    tall_sum = contract(place, operand, (0, 1), tall_first, split=width)
    far_left, far_right, tall_sum = lax.optimization_barrier((far_left, far_right, tall_sum))
    tall_third = [
        (hop(halves(far_left)[0], 0, 1), far_split[0]),
        (hop(halves(far_right)[1], 0, -1), far_split[1]),
    ]

    wide_rows = {dz: [(dz, dx, 0, BLOCK) for dx in X_ORDER] for dz in range(-4, 5)}
    wide_first = [(wide, wide_rows[0])]
    below = above = wide
    for distance in (1, 2):
        below, above = hop(below, 1, 0), hop(above, -1, 0)
        wide_first += [(below, wide_rows[-distance]), (above, wide_rows[distance])]
    wide_sum = contract(place, operand, (1,), wide_first)
    below, above = hop(below, 1, 0), hop(above, -1, 0)
    below, above, wide_sum = lax.optimization_barrier((below, above, wide_sum))
    wide_second = [(below, wide_rows[-3]), (above, wide_rows[3])]
    wide_split = parts(wide_rows[4])
    wide_third = [
        (hop(halves(below)[0], 1, 0), wide_split[0]),
        (hop(halves(above)[1], -1, 0), wide_split[1]),
    ]

    tall_sum = contract(place, operand, (0, 1), tall_second, tall_sum, split=width)
    wide_sum = contract(place, operand, (1,), wide_second, wide_sum)
    qkv, low = contract(
        place, operand, (0, 1), tall_third, tall_sum, split=width, dtype=jnp.bfloat16
    )
    out = contract(place, operand, (1,), wide_third, wide_sum, low, dtype=jnp.bfloat16)
    return qkv, out


def solution(mesh):
    placed = (P("col", "row"), P("col", "row"), P("row", "col"), P("row", "col"))
    return jax.shard_map(
        body,
        mesh=mesh,
        in_specs=placed,
        out_specs=(P("row", "col"), P("row", "col")),
        check_vma=False,
    )
```

```python
import functools

import jax
import jax.numpy as jnp
from jax import lax
from jax.experimental import pallas as pl
from jax.experimental.pallas import tpu as pltpu
from jax.sharding import PartitionSpec as P

Z, X, Y, C = 8, 4, 4, 2
BLOCK = 64
FEATURES = 512
TILE = 256
SPLIT = 256

X_ORDER = (0, -1, 1, 2)
NEAR, FAR = (0, -1, 1), (-2, 2, -3, 3, 4)


def hop(value, dz, dx):
    pairs = [
        (z * X + x, ((z + dz) % Z) * X + (x + dx) % X) for z in range(Z) for x in range(X)
    ]
    return lax.ppermute(value, "row", pairs)


def hop_y(value, dy, swap=0):
    pairs = [(y * C + c, ((y + dy) % Y) * C + (c ^ swap)) for y in range(Y) for c in range(C)]
    return lax.ppermute(value, "col", pairs)


def halves(value):
    half = value.shape[0] // 2
    return value[:half], value[half:]


def arrange_kernel(groups, place_ref, mine_ref, other_ref, *refs):
    outs, (left, sems) = refs[: len(groups)], refs[len(groups) :]
    z, x, y, core = (place_ref[i] for i in range(4))
    at, copies = 0, []
    for rows, ops in groups:
        width = len(ops) * FEATURES
        for dz, dx, start, size in rows:
            group = lax.rem(z + (dz + Z), Z)
            away = lax.rem(group // C + Y - y, Y)
            slot = jnp.where(away == 0, 0, jnp.where(away == Y - 1, 1, jnp.where(away == 1, 2, 3)))
            row = slot * (X * BLOCK) + lax.rem(x + (dx + X), X) * BLOCK + start
            source = (pl.ds(pl.multiple_of(row, 32), size), pl.ds(ops[0] * FEATURES, width))
            target = left.at[pl.ds(at, size), pl.ds(0, width)]
            swapped, sem = lax.rem(group, C) != core, sems.at[len(copies)]

            @pl.when(swapped)
            def _():
                pltpu.make_async_copy(other_ref.at[source], target, sem).start()

            @pl.when(jnp.logical_not(swapped))
            def _():
                pltpu.make_async_copy(mine_ref.at[source], target, sem).start()

            copies.append(pltpu.make_async_copy(target, target, sem))
            at += size
    at = 0
    for (rows, ops), out in zip(groups, outs):
        size = depth_of(rows)
        for _ in rows:
            copies.pop(0).wait()
        for i in range(len(ops)):
            out[i] = left[at : at + size, i * FEATURES : (i + 1) * FEATURES].T
        at += size


def arrange(place, operand, groups):
    anywhere = pl.BlockSpec(memory_space=pl.ANY)
    depth = sum(depth_of(rows) for rows, _ in groups)
    return pl.pallas_call(
        functools.partial(arrange_kernel, groups),
        out_shape=[
            jax.ShapeDtypeStruct((len(ops), FEATURES, depth_of(rows)), jnp.bfloat16)
            for rows, ops in groups
        ],
        in_specs=[pl.BlockSpec(memory_space=pltpu.SMEM), anywhere, anywhere],
        out_specs=[pl.BlockSpec(memory_space=pltpu.VMEM)] * len(groups),
        scratch_shapes=[
            pltpu.VMEM((depth, 2 * FEATURES), jnp.bfloat16),
            pltpu.SemaphoreType.DMA((sum(len(rows) for rows, _ in groups),)),
        ],
        compiler_params=pltpu.CompilerParams(vmem_limit_bytes=24 << 20),
        cost_estimate=pl.CostEstimate(flops=0, bytes_accessed=16 << 20, transcendentals=0),
    )(place, *operand)


def kernel(sizes, added, cut, ahead, left_ref, *refs):
    grads, refs = refs[: len(sizes)], refs[len(sizes) :]
    if added:
        total_ref, *refs = refs
    if ahead:
        prefix_ref, *refs = refs
    *outs, right = refs
    tile = pl.program_id(0)

    def work(out_ref):
        at = 0
        for grad, size in zip(grads, sizes):
            right[pl.ds(at, size)] = grad[...]
            at += size
        part = jnp.dot(left_ref[0], right[...], preferred_element_type=jnp.float32)
        if added:
            part += total_ref[...]
        out_ref[...] = part.astype(out_ref.dtype)

    if ahead:
        pl.when(tile < ahead)(lambda: outs[0].__setitem__(..., prefix_ref[...]))
        pl.when(tile >= ahead)(lambda: work(outs[0]))
    elif len(outs) == 1:
        work(outs[0])
    else:
        pl.when(tile < cut)(lambda: work(outs[0]))
        pl.when(tile >= cut)(lambda: work(outs[1]))


def contract(left, grads, total=None, prefix=None, split=None, dtype=jnp.float32):
    sizes = [array.shape[0] for array in grads]
    depth, width = sum(sizes), grads[0].shape[1]
    assert depth == left.shape[2]
    ahead = 0 if prefix is None else prefix.shape[1] // TILE
    tiles = ahead + width // TILE
    cut = tiles if split is None else split // TILE
    here = lambda height: pl.BlockSpec((height, TILE), lambda t: (0, jnp.maximum(t - ahead, 0)))
    if dtype == jnp.float32 or split is None:
        widths, specs = [tiles * TILE], [pl.BlockSpec((FEATURES, TILE), lambda t: (0, t))]
    else:
        widths = [cut * TILE, (tiles - cut) * TILE]
        specs = [
            pl.BlockSpec((FEATURES, TILE), lambda t: (0, jnp.minimum(t, cut - 1))),
            pl.BlockSpec((FEATURES, TILE), lambda t: (0, jnp.maximum(t - cut, 0))),
        ]
    extra, extra_specs = [], []
    if total is not None:
        extra, extra_specs = [total], [here(FEATURES)]
    if prefix is not None:
        extra.append(prefix)
        extra_specs.append(
            pl.BlockSpec((FEATURES, TILE), lambda t: (0, jnp.minimum(t, ahead - 1)))
        )
    results = pl.pallas_call(
        functools.partial(kernel, sizes, total is not None, cut, ahead),
        grid=(tiles,),
        out_shape=[jax.ShapeDtypeStruct((FEATURES, w), dtype) for w in widths],
        in_specs=[pl.BlockSpec((1, FEATURES, depth), lambda t: (jnp.where(t >= cut, 1, 0), 0, 0))]
        + [here(size) for size in sizes]
        + extra_specs,
        out_specs=specs,
        scratch_shapes=[pltpu.VMEM((depth, TILE), jnp.bfloat16)],
        compiler_params=pltpu.CompilerParams(vmem_limit_bytes=16 << 20),
        cost_estimate=pl.CostEstimate(
            flops=2 * FEATURES * depth * width,
            bytes_accessed=2 * depth * (width + FEATURES) + 4 * FEATURES * width,
            transcendentals=0,
        ),
    )(left, *grads, *extra)
    return results if len(results) > 1 else results[0]


def depth_of(rows):
    return sum(row[3] for row in rows)


def whole(dzs, dx):
    return [(dz, dx, 0, BLOCK) for dz in dzs]


def parts(rows):
    half, first, second = depth_of(rows) // 2, [], []
    for dz, dx, start, size in rows:
        here = min(size, half)
        if here:
            first.append((dz, dx, start, here))
        if here < size:
            second.append((dz, dx, start + here, size - here))
        half -= here
    return first, second


def body(normed_input, attended, qkv_grad, proj_grad):
    row, col = lax.axis_index("row"), lax.axis_index("col")
    place = jnp.stack([row // X, row % X, col // C, col % C])

    tall = jnp.concatenate([qkv_grad, proj_grad[:, :SPLIT]], axis=1)
    wide = proj_grad[:, SPLIT:]

    below, above = hop(tall, 1, 0), hop(tall, -1, 0)
    left, right, opposite = hop(wide, 0, 1), hop(wide, 0, -1), hop(wide, 0, 2)
    below, above, left, right, opposite = lax.optimization_barrier(
        (below, above, left, right, opposite)
    )
    near = jnp.concatenate([tall, below, above])
    near_left, near_right = hop(near, 0, 1), hop(near, 0, -1)
    far = []
    for distance in (2, 3):
        below, above = hop(below, 1, 0), hop(above, -1, 0)
        far += [below, above]
    below, above, near_left, near_right = lax.optimization_barrier(
        (below, above, near_left, near_right)
    )
    far[2:] = [below, above, hop(halves(below)[0], 1, 0), hop(halves(above)[1], -1, 0)]
    wide = jnp.concatenate([wide, left, right, opposite])

    mine = jnp.concatenate([normed_input, attended], axis=1)
    mine, opposite = lax.optimization_barrier((mine, opposite))
    down = hop_y(mine, 1)
    mine, down = lax.optimization_barrier((mine, down))
    up = hop_y(mine, -1)
    mine, up = lax.optimization_barrier((mine, up))
    mine = jnp.concatenate([mine, down, up, hop_y(mine, 2)])
    near_rows = {dx: whole(NEAR, dx) for dx in X_ORDER}
    far_rows = {dx: whole(FAR, dx) for dx in X_ORDER}
    near_split, far_split = parts(near_rows[2]), parts(far_rows[2])
    wide_rows = {dz: [(dz, dx, 0, BLOCK) for dx in X_ORDER] for dz in range(-4, 5)}
    wide_split = parts(wide_rows[4])
    groups = [
        (sum([near_rows[0], near_rows[-1], near_rows[1], *near_split, far_rows[0]], []), (0, 1)),
        (far_rows[-1] + far_rows[1], (0, 1)),
        (far_split[0] + far_split[1], (0, 1)),
        (sum([wide_rows[d] for d in (0, -1, 1, -2, 2)], []), (1,)),
        (wide_rows[-3] + wide_rows[3], (1,)),
        (wide_split[0] + wide_split[1], (1,)),
    ]
    lefts = arrange(place, (mine, hop_y(mine, 0, 1)), groups)

    far, wide, below, above = lax.optimization_barrier((far, wide, below, above))
    near_halves = [hop(halves(near_left)[0], 0, 1), hop(halves(near_right)[1], 0, -1)]
    far = jnp.concatenate(far)
    far, near_halves = lax.optimization_barrier((far, near_halves))
    far_left, far_right = hop(far, 0, 1), hop(far, 0, -1)
    width = qkv_grad.shape[1]
    tall_sum = contract(lefts[0], [near, near_left, near_right, *near_halves, far], split=width)

    below = above = wide
    wide_first = [wide]
    for distance in (1, 2):
        below, above = hop(below, 1, 0), hop(above, -1, 0)
        wide_first += [below, above]
    below, above, tall_sum = lax.optimization_barrier((below, above, tall_sum))
    wide_sum = contract(lefts[3], wide_first)
    below, above = hop(below, 1, 0), hop(above, -1, 0)
    far_left, far_right, tall_sum = lax.optimization_barrier((far_left, far_right, tall_sum))
    far_halves = [hop(halves(far_left)[0], 0, 1), hop(halves(far_right)[1], 0, -1)]
    below, above, wide_sum = lax.optimization_barrier((below, above, wide_sum))
    wide_halves = [hop(halves(below)[0], 1, 0), hop(halves(above)[1], -1, 0)]

    tall_sum = contract(lefts[1], [far_left, far_right], tall_sum, split=width)
    wide_sum = contract(lefts[4], [below, above], wide_sum)
    qkv, low = contract(lefts[2], far_halves, tall_sum, split=width, dtype=jnp.bfloat16)
    out = contract(lefts[5], wide_halves, wide_sum, low, dtype=jnp.bfloat16)
    return qkv, out


def solution(mesh):
    placed = (P("col", "row"), P("col", "row"), P("row", "col"), P("row", "col"))
    return jax.shard_map(
        body,
        mesh=mesh,
        in_specs=placed,
        out_specs=(P("row", "col"), P("row", "col")),
        check_vma=False,
    )
```

```python
import functools

import jax
import jax.numpy as jnp
from jax import lax
from jax.experimental import pallas as pl
from jax.experimental.pallas import tpu as pltpu
from jax.sharding import PartitionSpec as P

Z, X, Y, C = 8, 4, 4, 2
BLOCK = 64
FEATURES = 512

X_ORDER = (0, -1, 1, 2)
NEAR, FAR = (0, -1, 1), (-2, 2, -3, 3, 4)


def hop(value, dz, dx):
    pairs = [
        (z * X + x, ((z + dz) % Z) * X + (x + dx) % X) for z in range(Z) for x in range(X)
    ]
    return lax.ppermute(value, "row", pairs)


def hop_y(value, dy, swap=0):
    pairs = [(y * C + c, ((y + dy) % Y) * C + (c ^ swap)) for y in range(Y) for c in range(C)]
    return lax.ppermute(value, "col", pairs)


def halves(value):
    half = value.shape[0] // 2
    return value[:half], value[half:]


def arrange_kernel(groups, place_ref, mine_ref, other_ref, *refs):
    outs, (left, sems) = refs[: len(groups)], refs[len(groups) :]
    z, x, y, core = (place_ref[i] for i in range(4))
    at, copies = 0, []
    for rows, op in groups:
        for dz, dx, start, size in rows:
            group = lax.rem(z + (dz + Z), Z)
            away = lax.rem(group // C + Y - y, Y)
            slot = jnp.where(away == 0, 0, jnp.where(away == Y - 1, 1, jnp.where(away == 1, 2, 3)))
            row = slot * (X * BLOCK) + lax.rem(x + (dx + X), X) * BLOCK + start
            source = (pl.ds(pl.multiple_of(row, 32), size), pl.ds(op * FEATURES, FEATURES))
            target = left.at[pl.ds(at, size)]
            swapped, sem = lax.rem(group, C) != core, sems.at[len(copies)]

            @pl.when(swapped)
            def _():
                pltpu.make_async_copy(other_ref.at[source], target, sem).start()

            @pl.when(jnp.logical_not(swapped))
            def _():
                pltpu.make_async_copy(mine_ref.at[source], target, sem).start()

            copies.append(pltpu.make_async_copy(target, target, sem))
            at += size
    at = 0
    for (rows, _), out in zip(groups, outs):
        size = depth_of(rows)
        for _ in rows:
            copies.pop(0).wait()
        out[...] = left[at : at + size].T
        at += size


def arrange(place, operand, groups):
    anywhere = pl.BlockSpec(memory_space=pl.ANY)
    depth = sum(depth_of(rows) for rows, _ in groups)
    return pl.pallas_call(
        functools.partial(arrange_kernel, groups),
        out_shape=[
            jax.ShapeDtypeStruct((FEATURES, depth_of(rows)), jnp.bfloat16) for rows, _ in groups
        ],
        in_specs=[pl.BlockSpec(memory_space=pltpu.SMEM), anywhere, anywhere],
        out_specs=[pl.BlockSpec(memory_space=pltpu.VMEM)] * len(groups),
        scratch_shapes=[
            pltpu.VMEM((depth, FEATURES), jnp.bfloat16),
            pltpu.SemaphoreType.DMA((sum(len(rows) for rows, _ in groups),)),
        ],
        compiler_params=pltpu.CompilerParams(vmem_limit_bytes=16 << 20),
        cost_estimate=pl.CostEstimate(flops=0, bytes_accessed=12 << 20, transcendentals=0),
    )(place, *operand)


def contract(left, grads, total=None, dtype=jnp.float32):
    part = jnp.dot(left, jnp.concatenate(grads), preferred_element_type=jnp.float32)
    if total is not None:
        part += total
    return part.astype(dtype)


def depth_of(rows):
    return sum(row[3] for row in rows)


def whole(dzs, dx):
    return [(dz, dx, 0, BLOCK) for dz in dzs]


def parts(rows):
    half, first, second = depth_of(rows) // 2, [], []
    for dz, dx, start, size in rows:
        here = min(size, half)
        if here:
            first.append((dz, dx, start, here))
        if here < size:
            second.append((dz, dx, start + here, size - here))
        half -= here
    return first, second


def body(normed_input, attended, qkv_grad, proj_grad):
    together = lax.optimization_barrier
    row, col = lax.axis_index("row"), lax.axis_index("col")
    place = jnp.stack([row // X, row % X, col // C, col % C])

    tall, wide = qkv_grad, proj_grad
    mine = jnp.concatenate([normed_input, attended], axis=1)

    below, above = hop(tall, 1, 0), hop(tall, -1, 0)
    left, right = hop(wide, 0, 1), hop(wide, 0, -1)
    down = hop_y(mine, 1)
    below, above, left, right = together((below, above, left, right))
    opposite = hop(wide, 0, 2)
    near = jnp.concatenate([tall, below, above])
    near, opposite = together((near, opposite))
    near_left, near_right = hop(near, 0, 1), hop(near, 0, -1)
    below, above = hop(below, 1, 0), hop(above, -1, 0)
    below, above, opposite, down = together((below, above, opposite, down))
    far = [below, above]
    below, above = hop(below, 1, 0), hop(above, -1, 0)
    far = jnp.concatenate([*far, below, above])
    mine, down = together((mine, down))
    up = hop_y(mine, -1)
    below, above, near_left, near_right, far, up = together(
        (below, above, near_left, near_right, far, up)
    )
    mine, up = together((mine, up))
    across = hop_y(mine, 2)
    far = [far, hop(halves(below)[0], 1, 0), hop(halves(above)[1], -1, 0)]
    near_halves = [hop(halves(near_left)[0], 0, 1), hop(halves(near_right)[1], 0, -1)]
    wide = jnp.concatenate([wide, left, right, opposite])
    far, wide = together((far, wide))
    far = jnp.concatenate(far)
    far, near_halves, across = together((far, near_halves, across))
    far_left, far_right = hop(far, 0, 1), hop(far, 0, -1)
    below, above = hop(wide, 1, 0), hop(wide, -1, 0)
    wide_first = [wide, below, above]
    mine = jnp.concatenate([mine, down, up, across])

    near_rows = {dx: whole(NEAR, dx) for dx in X_ORDER}
    far_rows = {dx: whole(FAR, dx) for dx in X_ORDER}
    near_split, far_split = parts(near_rows[2]), parts(far_rows[2])
    wide_rows = {dz: [(dz, dx, 0, BLOCK) for dx in X_ORDER] for dz in range(-4, 5)}
    wide_split = parts(wide_rows[4])
    groups = [
        (sum([near_rows[0], near_rows[-1], near_rows[1], *near_split, far_rows[0]], []), 0),
        (far_rows[-1] + far_rows[1], 0),
        (far_split[0] + far_split[1], 0),
        (sum([wide_rows[d] for d in (0, -1, 1, -2, 2)], []), 1),
        (wide_rows[-3] + wide_rows[3], 1),
        (wide_split[0] + wide_split[1], 1),
    ]
    lefts = arrange(place, (mine, hop_y(mine, 0, 1)), groups)
    tall_sum = contract(lefts[0], [near, near_left, near_right, *near_halves, far])

    below, above = hop(below, 1, 0), hop(above, -1, 0)
    wide_first += [below, above]
    below, above, far_left, far_right, tall_sum = together(
        (below, above, far_left, far_right, tall_sum)
    )
    wide_sum = contract(lefts[3], wide_first)
    below, above = hop(below, 1, 0), hop(above, -1, 0)
    far_halves = [hop(halves(far_left)[0], 0, 1), hop(halves(far_right)[1], 0, -1)]
    below, above, wide_sum = together((below, above, wide_sum))
    wide_halves = [hop(halves(below)[0], 1, 0), hop(halves(above)[1], -1, 0)]

    tall_sum = contract(lefts[1], [far_left, far_right], tall_sum)
    wide_sum = contract(lefts[4], [below, above], wide_sum)
    qkv = contract(lefts[2], far_halves, tall_sum, dtype=jnp.bfloat16)
    out = contract(lefts[5], wide_halves, wide_sum, dtype=jnp.bfloat16)
    return qkv, out


def solution(mesh):
    placed = (P("col", "row"), P("col", "row"), P("row", "col"), P("row", "col"))
    return jax.shard_map(
        body,
        mesh=mesh,
        in_specs=placed,
        out_specs=(P("row", "col"), P("row", "col")),
        check_vma=False,
    )
```

```python
import functools

import jax
import jax.numpy as jnp
from jax import lax
from jax.experimental import pallas as pl
from jax.experimental.pallas import tpu as pltpu
from jax.sharding import PartitionSpec as P

Z, X, Y, C = 8, 4, 4, 2
BLOCK = 64
FEATURES = 512

X_ORDER = (0, -1, 1, 2)
NEAR, FAR = (0, -1, 1), (-2, 2, -3, 3, 4)


def hop(value, dz, dx):
    pairs = [
        (z * X + x, ((z + dz) % Z) * X + (x + dx) % X) for z in range(Z) for x in range(X)
    ]
    return lax.ppermute(value, "row", pairs)


def hop_y(value, dy, swap=0):
    pairs = [(y * C + c, ((y + dy) % Y) * C + (c ^ swap)) for y in range(Y) for c in range(C)]
    return lax.ppermute(value, "col", pairs)


def halves(value):
    half = value.shape[0] // 2
    return value[:half], value[half:]


def arrange_kernel(groups, place_ref, mine_ref, other_ref, *refs):
    outs, (left, sems) = refs[: len(groups)], refs[len(groups) :]
    z, x, y, core = (place_ref[i] for i in range(4))
    at, copies = 0, []
    for rows, op in groups:
        for dz, dx, start, size in rows:
            group = lax.rem(z + (dz + Z), Z)
            away = lax.rem(group // C + Y - y, Y)
            slot = jnp.where(away == 0, 0, jnp.where(away == Y - 1, 1, jnp.where(away == 1, 2, 3)))
            row = slot * (X * BLOCK) + lax.rem(x + (dx + X), X) * BLOCK + start
            source = (pl.ds(pl.multiple_of(row, 32), size), pl.ds(op * FEATURES, FEATURES))
            target = left.at[pl.ds(at, size)]
            swapped, sem = lax.rem(group, C) != core, sems.at[len(copies)]

            @pl.when(swapped)
            def _():
                pltpu.make_async_copy(other_ref.at[source], target, sem).start()

            @pl.when(jnp.logical_not(swapped))
            def _():
                pltpu.make_async_copy(mine_ref.at[source], target, sem).start()

            copies.append(pltpu.make_async_copy(target, target, sem))
            at += size
    at = 0
    for (rows, _), out in zip(groups, outs):
        size = depth_of(rows)
        for _ in rows:
            copies.pop(0).wait()
        out[...] = left[at : at + size].T
        at += size


def arrange(place, operand, groups):
    anywhere = pl.BlockSpec(memory_space=pl.ANY)
    depth = sum(depth_of(rows) for rows, _ in groups)
    return pl.pallas_call(
        functools.partial(arrange_kernel, groups),
        out_shape=[
            jax.ShapeDtypeStruct((FEATURES, depth_of(rows)), jnp.bfloat16) for rows, _ in groups
        ],
        in_specs=[pl.BlockSpec(memory_space=pltpu.SMEM), anywhere, anywhere],
        out_specs=[pl.BlockSpec(memory_space=pltpu.VMEM)] * len(groups),
        scratch_shapes=[
            pltpu.VMEM((depth, FEATURES), jnp.bfloat16),
            pltpu.SemaphoreType.DMA((sum(len(rows) for rows, _ in groups),)),
        ],
        compiler_params=pltpu.CompilerParams(vmem_limit_bytes=16 << 20),
        cost_estimate=pl.CostEstimate(flops=0, bytes_accessed=12 << 20, transcendentals=0),
    )(place, *operand)


def contract(left, grads, total=None, dtype=jnp.float32):
    part = jnp.dot(left, jnp.concatenate(grads), preferred_element_type=jnp.float32)
    if total is not None:
        part += total
    return part.astype(dtype)


def depth_of(rows):
    return sum(row[3] for row in rows)


def whole(dzs, dx):
    return [(dz, dx, 0, BLOCK) for dz in dzs]


def parts(rows):
    half, first, second = depth_of(rows) // 2, [], []
    for dz, dx, start, size in rows:
        here = min(size, half)
        if here:
            first.append((dz, dx, start, here))
        if here < size:
            second.append((dz, dx, start + here, size - here))
        half -= here
    return first, second


def body(normed_input, attended, qkv_grad, proj_grad):
    together = lax.optimization_barrier
    row, col = lax.axis_index("row"), lax.axis_index("col")
    place = jnp.stack([row // X, row % X, col // C, col % C])

    tall, wide = qkv_grad, proj_grad
    mine = jnp.concatenate([normed_input, attended], axis=1)

    below, above = hop(tall, 1, 0), hop(tall, -1, 0)
    left, right = hop(wide, 0, 1), hop(wide, 0, -1)
    down = hop_y(mine, 1)
    below, above, left, right = together((below, above, left, right))
    opposite = hop(wide, 0, 2)
    near = jnp.concatenate([tall, below, above])
    near, opposite = together((near, opposite))
    near_left, near_right = hop(near, 0, 1), hop(near, 0, -1)
    below, above = hop(below, 1, 0), hop(above, -1, 0)
    below, above, opposite, mine, down = together((below, above, opposite, mine, down))
    up = hop_y(mine, -1)
    far = [below, above]
    below, above = hop(below, 1, 0), hop(above, -1, 0)
    far = jnp.concatenate([*far, below, above])
    below, above, far = together((below, above, far))
    mine, up = together((mine, up))
    across = hop_y(mine, 2)
    far = [far, hop(halves(below)[0], 1, 0), hop(halves(above)[1], -1, 0)]
    wide = jnp.concatenate([wide, left, right, opposite])
    far, wide, near_left, near_right = together((far, wide, near_left, near_right))
    near_halves = [hop(halves(near_left)[0], 0, 1), hop(halves(near_right)[1], 0, -1)]
    far = jnp.concatenate(far)
    far, near_halves, across = together((far, near_halves, across))
    far_left, far_right = hop(far, 0, 1), hop(far, 0, -1)
    below, above = hop(wide, 1, 0), hop(wide, -1, 0)
    wide_first = [wide, below, above]
    mine = jnp.concatenate([mine, down, up, across])

    near_rows = {dx: whole(NEAR, dx) for dx in X_ORDER}
    far_rows = {dx: whole(FAR, dx) for dx in X_ORDER}
    near_split, far_split = parts(near_rows[2]), parts(far_rows[2])
    wide_rows = {dz: [(dz, dx, 0, BLOCK) for dx in X_ORDER] for dz in range(-4, 5)}
    wide_split = parts(wide_rows[4])
    groups = [
        (sum([near_rows[0], near_rows[-1], near_rows[1], *near_split, far_rows[0]], []), 0),
        (far_rows[-1] + far_rows[1], 0),
        (far_split[0] + far_split[1], 0),
        (sum([wide_rows[d] for d in (0, -1, 1, -2, 2)], []), 1),
        (wide_rows[-3] + wide_rows[3], 1),
        (wide_split[0] + wide_split[1], 1),
    ]
    lefts = arrange(place, (mine, hop_y(mine, 0, 1)), groups)
    tall_sum = contract(lefts[0], [near, near_left, near_right, *near_halves, far])

    below, above = hop(below, 1, 0), hop(above, -1, 0)
    wide_first += [below, above]
    below, above, far_left, far_right = together((below, above, far_left, far_right))
    wide_sum = contract(lefts[3], wide_first)
    below, above = hop(below, 1, 0), hop(above, -1, 0)
    far_halves = [hop(halves(far_left)[0], 0, 1), hop(halves(far_right)[1], 0, -1)]
    below, above, wide_sum = together((below, above, wide_sum))
    wide_halves = [hop(halves(below)[0], 1, 0), hop(halves(above)[1], -1, 0)]

    tall_sum = contract(lefts[1], [far_left, far_right], tall_sum)
    wide_sum = contract(lefts[4], [below, above], wide_sum)
    tall_sum, wide_sum = together((tall_sum, wide_sum))
    qkv = contract(lefts[2], far_halves, tall_sum, dtype=jnp.bfloat16)
    out = contract(lefts[5], wide_halves, wide_sum, dtype=jnp.bfloat16)
    return qkv, out


def solution(mesh):
    placed = (P("col", "row"), P("col", "row"), P("row", "col"), P("row", "col"))
    return jax.shard_map(
        body,
        mesh=mesh,
        in_specs=placed,
        out_specs=(P("row", "col"), P("row", "col")),
        check_vma=False,
    )
```

```python
import functools

import jax
import jax.numpy as jnp
from jax import lax
from jax.experimental import pallas as pl
from jax.experimental.pallas import tpu as pltpu
from jax.sharding import PartitionSpec as P

Z, X, Y, C = 8, 4, 4, 2
BLOCK = 64
FEATURES = 512

X_ORDER = (0, -1, 1, 2)
NEAR, FAR = (0, -1, 1), (-2, 2, -3, 3, 4)


def hop(value, dz, dx):
    pairs = [
        (z * X + x, ((z + dz) % Z) * X + (x + dx) % X) for z in range(Z) for x in range(X)
    ]
    return lax.ppermute(value, "row", pairs)


def hop_y(value, dy, swap=0):
    pairs = [(y * C + c, ((y + dy) % Y) * C + (c ^ swap)) for y in range(Y) for c in range(C)]
    return lax.ppermute(value, "col", pairs)


def halves(value):
    half = value.shape[0] // 2
    return value[:half], value[half:]


def arrange_kernel(groups, place_ref, mine_ref, other_ref, *refs):
    outs, (left, sems) = refs[: len(groups)], refs[len(groups) :]
    z, x, y, core = (place_ref[i] for i in range(4))
    at, copies = 0, []
    for rows, op in groups:
        for dz, dx, start, size in rows:
            group = lax.rem(z + (dz + Z), Z)
            away = lax.rem(group // C + Y - y, Y)
            slot = jnp.where(away == 0, 0, jnp.where(away == Y - 1, 1, jnp.where(away == 1, 2, 3)))
            row = slot * (X * BLOCK) + lax.rem(x + (dx + X), X) * BLOCK + start
            source = (pl.ds(pl.multiple_of(row, 32), size), pl.ds(op * FEATURES, FEATURES))
            target = left.at[pl.ds(at, size)]
            swapped, sem = lax.rem(group, C) != core, sems.at[len(copies)]

            @pl.when(swapped)
            def _():
                pltpu.make_async_copy(other_ref.at[source], target, sem).start()

            @pl.when(jnp.logical_not(swapped))
            def _():
                pltpu.make_async_copy(mine_ref.at[source], target, sem).start()

            copies.append(pltpu.make_async_copy(target, target, sem))
            at += size
    at = 0
    for (rows, _), out in zip(groups, outs):
        size = depth_of(rows)
        for _ in rows:
            copies.pop(0).wait()
        out[...] = left[at : at + size].T
        at += size


def arrange(place, operand, groups):
    anywhere = pl.BlockSpec(memory_space=pl.ANY)
    depth = sum(depth_of(rows) for rows, _ in groups)
    return pl.pallas_call(
        functools.partial(arrange_kernel, groups),
        out_shape=[
            jax.ShapeDtypeStruct((FEATURES, depth_of(rows)), jnp.bfloat16) for rows, _ in groups
        ],
        in_specs=[pl.BlockSpec(memory_space=pltpu.SMEM), anywhere, anywhere],
        out_specs=[pl.BlockSpec(memory_space=pltpu.VMEM)] * len(groups),
        scratch_shapes=[
            pltpu.VMEM((depth, FEATURES), jnp.bfloat16),
            pltpu.SemaphoreType.DMA((sum(len(rows) for rows, _ in groups),)),
        ],
        compiler_params=pltpu.CompilerParams(vmem_limit_bytes=16 << 20),
        cost_estimate=pl.CostEstimate(flops=0, bytes_accessed=12 << 20, transcendentals=0),
    )(place, *operand)


def contract(left, grads, total=None, dtype=jnp.float32):
    part = jnp.dot(left, jnp.concatenate(grads), preferred_element_type=jnp.float32)
    if total is not None:
        part += total
    return part.astype(dtype)


def depth_of(rows):
    return sum(row[3] for row in rows)


def whole(dzs, dx):
    return [(dz, dx, 0, BLOCK) for dz in dzs]


def parts(rows):
    half, first, second = depth_of(rows) // 2, [], []
    for dz, dx, start, size in rows:
        here = min(size, half)
        if here:
            first.append((dz, dx, start, here))
        if here < size:
            second.append((dz, dx, start + here, size - here))
        half -= here
    return first, second


def body(normed_input, attended, qkv_grad, proj_grad):
    together = lax.optimization_barrier
    row, col = lax.axis_index("row"), lax.axis_index("col")
    place = jnp.stack([row // X, row % X, col // C, col % C])

    tall, wide = qkv_grad, proj_grad
    mine = jnp.concatenate([normed_input, attended], axis=1)

    below, above = hop(tall, 1, 0), hop(tall, -1, 0)
    left, right = hop(wide, 0, 1), hop(wide, 0, -1)
    down = hop_y(mine, 1)
    below, above, left, right = together((below, above, left, right))
    opposite = hop(wide, 0, 2)
    near = jnp.concatenate([tall, below, above])
    near, opposite = together((near, opposite))
    near_left, near_right = hop(near, 0, 1), hop(near, 0, -1)
    below, above = hop(below, 1, 0), hop(above, -1, 0)
    below, above, opposite, mine, down = together((below, above, opposite, mine, down))
    up = hop_y(mine, -1)
    far = [below, above]
    below, above = hop(below, 1, 0), hop(above, -1, 0)
    far = jnp.concatenate([*far, below, above])
    below, above, far = together((below, above, far))
    mine, up, near_left, near_right = together((mine, up, near_left, near_right))
    across = hop_y(mine, 2)
    far = [far, hop(halves(below)[0], 1, 0), hop(halves(above)[1], -1, 0)]
    wide = jnp.concatenate([wide, left, right, opposite])
    far, wide = together((far, wide))
    far = jnp.concatenate(far)
    far, near_left, near_right = together((far, near_left, near_right))
    far_left, far_right = hop(far, 0, 1), hop(far, 0, -1)
    below, above = hop(wide, 1, 0), hop(wide, -1, 0)
    wide_first = [wide, below, above]
    tall_first = [near, near_left, near_right, far]
    below, above, tall_first = together((below, above, tall_first))
    mine = jnp.concatenate([mine, down, up, across])

    near_rows = {dx: whole(NEAR, dx) for dx in X_ORDER}
    far_rows = {dx: whole(FAR, dx) for dx in X_ORDER}
    near_split, far_split = parts(near_rows[2]), parts(far_rows[2])
    wide_rows = {dz: [(dz, dx, 0, BLOCK) for dx in X_ORDER] for dz in range(-4, 5)}
    wide_split = parts(wide_rows[4])
    groups = [
        (sum([near_rows[0], near_rows[-1], near_rows[1], far_rows[0]], []), 0),
        (far_rows[-1] + far_rows[1], 0),
        (near_split[0] + far_split[0] + near_split[1] + far_split[1], 0),
        (wide_rows[0] + wide_rows[-1] + wide_rows[1], 1),
        (sum([wide_rows[d] for d in (-2, 2, -3, 3)], []), 1),
        (wide_split[0] + wide_split[1], 1),
    ]
    lefts = arrange(place, (mine, hop_y(mine, 0, 1)), groups)
    tall_sum = contract(lefts[0], tall_first)

    below, above = hop(below, 1, 0), hop(above, -1, 0)
    wide_second = [below, above]
    below, above, far_left, far_right = together((below, above, far_left, far_right))
    wide_sum = contract(lefts[3], wide_first)
    below, above = hop(below, 1, 0), hop(above, -1, 0)
    first = jnp.concatenate([halves(near_left)[0], halves(far_left)[0]])
    second = jnp.concatenate([halves(near_right)[1], halves(far_right)[1]])
    tall_halves = [hop(first, 0, 1), hop(second, 0, -1)]
    below, above, wide_sum = together((below, above, wide_sum))
    wide_halves = [hop(halves(below)[0], 1, 0), hop(halves(above)[1], -1, 0)]

    tall_sum = contract(lefts[1], [far_left, far_right], tall_sum)
    wide_sum = contract(lefts[4], [*wide_second, below, above], wide_sum)
    tall_sum, wide_sum = together((tall_sum, wide_sum))
    qkv = contract(lefts[2], tall_halves, tall_sum, dtype=jnp.bfloat16)
    out = contract(lefts[5], wide_halves, wide_sum, dtype=jnp.bfloat16)
    return qkv, out


def solution(mesh):
    placed = (P("col", "row"), P("col", "row"), P("row", "col"), P("row", "col"))
    return jax.shard_map(
        body,
        mesh=mesh,
        in_specs=placed,
        out_specs=(P("row", "col"), P("row", "col")),
        check_vma=False,
    )
```

```python
import functools

import jax
import jax.numpy as jnp
from jax import lax
from jax.experimental import pallas as pl
from jax.experimental.pallas import tpu as pltpu
from jax.sharding import PartitionSpec as P

Z, X, Y, C = 8, 4, 4, 2
BLOCK = 64
FEATURES = 512

X_ORDER = (0, -1, 1, 2)
NEAR, FAR = (0, -1, 1), (-2, 2, -3, 3, 4)


def hop(value, dz, dx):
    pairs = [
        (z * X + x, ((z + dz) % Z) * X + (x + dx) % X) for z in range(Z) for x in range(X)
    ]
    return lax.ppermute(value, "row", pairs)


def hop_y(value, dy, swap=0):
    pairs = [(y * C + c, ((y + dy) % Y) * C + (c ^ swap)) for y in range(Y) for c in range(C)]
    return lax.ppermute(value, "col", pairs)


def halves(value):
    half = value.shape[0] // 2
    return value[:half], value[half:]


def arrange_kernel(groups, place_ref, mine_ref, other_ref, *refs):
    outs, (left, sems) = refs[: len(groups)], refs[len(groups) :]
    z, x, y, core = (place_ref[i] for i in range(4))
    at, copies = 0, []
    for rows, op in groups:
        for dz, dx, start, size in rows:
            group = lax.rem(z + (dz + Z), Z)
            away = lax.rem(group // C + Y - y, Y)
            slot = jnp.where(away == 0, 0, jnp.where(away == Y - 1, 1, jnp.where(away == 1, 2, 3)))
            row = slot * (X * BLOCK) + lax.rem(x + (dx + X), X) * BLOCK + start
            source = (pl.ds(pl.multiple_of(row, 32), size), pl.ds(op * FEATURES, FEATURES))
            target = left.at[pl.ds(at, size)]
            swapped, sem = lax.rem(group, C) != core, sems.at[len(copies)]

            @pl.when(swapped)
            def _():
                pltpu.make_async_copy(other_ref.at[source], target, sem).start()

            @pl.when(jnp.logical_not(swapped))
            def _():
                pltpu.make_async_copy(mine_ref.at[source], target, sem).start()

            copies.append(pltpu.make_async_copy(target, target, sem))
            at += size
    at = 0
    for (rows, _), out in zip(groups, outs):
        size = depth_of(rows)
        for _ in rows:
            copies.pop(0).wait()
        out[...] = left[at : at + size].T
        at += size


def arrange(place, operand, groups):
    anywhere = pl.BlockSpec(memory_space=pl.ANY)
    depth = sum(depth_of(rows) for rows, _ in groups)
    return pl.pallas_call(
        functools.partial(arrange_kernel, groups),
        out_shape=[
            jax.ShapeDtypeStruct((FEATURES, depth_of(rows)), jnp.bfloat16) for rows, _ in groups
        ],
        in_specs=[pl.BlockSpec(memory_space=pltpu.SMEM), anywhere, anywhere],
        out_specs=[pl.BlockSpec(memory_space=pltpu.VMEM)] * len(groups),
        scratch_shapes=[
            pltpu.VMEM((depth, FEATURES), jnp.bfloat16),
            pltpu.SemaphoreType.DMA((sum(len(rows) for rows, _ in groups),)),
        ],
        compiler_params=pltpu.CompilerParams(vmem_limit_bytes=16 << 20),
        cost_estimate=pl.CostEstimate(flops=0, bytes_accessed=12 << 20, transcendentals=0),
    )(place, *operand)


def contract(left, grads, total=None, dtype=jnp.float32):
    part = jnp.dot(left, jnp.concatenate(grads), preferred_element_type=jnp.float32)
    if total is not None:
        part += total
    return part.astype(dtype)


def depth_of(rows):
    return sum(row[3] for row in rows)


def whole(dzs, dx):
    return [(dz, dx, 0, BLOCK) for dz in dzs]


def parts(rows):
    half, first, second = depth_of(rows) // 2, [], []
    for dz, dx, start, size in rows:
        here = min(size, half)
        if here:
            first.append((dz, dx, start, here))
        if here < size:
            second.append((dz, dx, start + here, size - here))
        half -= here
    return first, second


def body(normed_input, attended, qkv_grad, proj_grad):
    together = lax.optimization_barrier
    row, col = lax.axis_index("row"), lax.axis_index("col")
    place = jnp.stack([row // X, row % X, col // C, col % C])

    tall, wide = qkv_grad, proj_grad
    mine = jnp.concatenate([normed_input, attended], axis=1)

    below, above = hop(tall, 1, 0), hop(tall, -1, 0)
    left, right, opposite = hop(wide, 0, 1), hop(wide, 0, -1), hop(wide, 0, 2)
    near = jnp.concatenate([tall, below, above])
    near, opposite = together((near, opposite))
    near_left, near_right = hop(near, 0, 1), hop(near, 0, -1)
    below, above = hop(below, 1, 0), hop(above, -1, 0)
    below, above, left, right = together((below, above, left, right))
    far = [below, above]
    below, above = hop(below, 1, 0), hop(above, -1, 0)
    far = jnp.concatenate([*far, below, above])
    down = hop_y(mine, 1)
    below, above, far = together((below, above, far))
    mine, down = together((mine, down))
    up = hop_y(mine, -1)
    mine, up, near_left, near_right = together((mine, up, near_left, near_right))
    across = hop_y(mine, 2)
    far = [far, hop(halves(below)[0], 1, 0), hop(halves(above)[1], -1, 0)]
    wide = jnp.concatenate([wide, left, right, opposite])
    far, wide = together((far, wide))
    far = jnp.concatenate(far)
    far, near_left, near_right = together((far, near_left, near_right))
    far_left, far_right = hop(far, 0, 1), hop(far, 0, -1)
    below, above = hop(wide, 1, 0), hop(wide, -1, 0)
    wide_first = [wide, below, above]
    tall_first = [near, near_left, near_right, far]
    below, above, tall_first = together((below, above, tall_first))
    mine = jnp.concatenate([mine, down, up, across])

    near_rows = {dx: whole(NEAR, dx) for dx in X_ORDER}
    far_rows = {dx: whole(FAR, dx) for dx in X_ORDER}
    near_split, far_split = parts(near_rows[2]), parts(far_rows[2])
    wide_rows = {dz: [(dz, dx, 0, BLOCK) for dx in X_ORDER] for dz in range(-4, 5)}
    wide_split = parts(wide_rows[4])
    groups = [
        (sum([near_rows[0], near_rows[-1], near_rows[1], far_rows[0]], []), 0),
        (far_rows[-1] + far_rows[1], 0),
        (near_split[0] + far_split[0] + near_split[1] + far_split[1], 0),
        (wide_rows[0] + wide_rows[-1] + wide_rows[1], 1),
        (sum([wide_rows[d] for d in (-2, 2, -3, 3)], []), 1),
        (wide_split[0] + wide_split[1], 1),
    ]
    lefts = arrange(place, (mine, hop_y(mine, 0, 1)), groups)
    tall_sum = contract(lefts[0], tall_first)

    below, above = hop(below, 1, 0), hop(above, -1, 0)
    wide_second = [below, above]
    below, above, far_left, far_right = together((below, above, far_left, far_right))
    wide_sum = contract(lefts[3], wide_first)
    below, above = hop(below, 1, 0), hop(above, -1, 0)
    first = jnp.concatenate([halves(near_left)[0], halves(far_left)[0]])
    second = jnp.concatenate([halves(near_right)[1], halves(far_right)[1]])
    tall_halves = [hop(first, 0, 1), hop(second, 0, -1)]
    below, above, wide_sum = together((below, above, wide_sum))
    wide_halves = [hop(halves(below)[0], 1, 0), hop(halves(above)[1], -1, 0)]

    tall_sum = contract(lefts[1], [far_left, far_right], tall_sum)
    wide_sum = contract(lefts[4], [*wide_second, below, above], wide_sum)
    tall_sum, wide_sum = together((tall_sum, wide_sum))
    qkv = contract(lefts[2], tall_halves, tall_sum, dtype=jnp.bfloat16)
    out = contract(lefts[5], wide_halves, wide_sum, dtype=jnp.bfloat16)
    return qkv, out


def solution(mesh):
    placed = (P("col", "row"), P("col", "row"), P("row", "col"), P("row", "col"))
    return jax.shard_map(
        body,
        mesh=mesh,
        in_specs=placed,
        out_specs=(P("row", "col"), P("row", "col")),
        check_vma=False,
    )
```

```python
import functools

import jax
import jax.numpy as jnp
from jax import lax
from jax.experimental import pallas as pl
from jax.experimental.pallas import tpu as pltpu
from jax.sharding import PartitionSpec as P

Z, X, Y, C = 8, 4, 4, 2
BLOCK = 64
FEATURES = 512

X_ORDER = (0, -1, 1, 2)
NEAR, FAR = (0, -1, 1), (-2, 2, -3, 3, 4)


def hop(value, dz, dx):
    pairs = [
        (z * X + x, ((z + dz) % Z) * X + (x + dx) % X) for z in range(Z) for x in range(X)
    ]
    return lax.ppermute(value, "row", pairs)


def hop_y(value, dy, swap=0):
    pairs = [(y * C + c, ((y + dy) % Y) * C + (c ^ swap)) for y in range(Y) for c in range(C)]
    return lax.ppermute(value, "col", pairs)


def halves(value):
    half = value.shape[0] // 2
    return value[:half], value[half:]


def arrange_kernel(groups, place_ref, mine_ref, other_ref, *refs):
    outs, (left, sems) = refs[: len(groups)], refs[len(groups) :]
    z, x, y, core = (place_ref[i] for i in range(4))
    at, copies = 0, []
    for rows, op in groups:
        for dz, dx, start, size in rows:
            group = lax.rem(z + (dz + Z), Z)
            away = lax.rem(group // C + Y - y, Y)
            slot = jnp.where(away == 0, 0, jnp.where(away == Y - 1, 1, jnp.where(away == 1, 2, 3)))
            row = slot * (X * BLOCK) + lax.rem(x + (dx + X), X) * BLOCK + start
            source = (pl.ds(pl.multiple_of(row, 32), size), pl.ds(op * FEATURES, FEATURES))
            target = left.at[pl.ds(at, size)]
            swapped, sem = lax.rem(group, C) != core, sems.at[len(copies)]

            @pl.when(swapped)
            def _():
                pltpu.make_async_copy(other_ref.at[source], target, sem).start()

            @pl.when(jnp.logical_not(swapped))
            def _():
                pltpu.make_async_copy(mine_ref.at[source], target, sem).start()

            copies.append(pltpu.make_async_copy(target, target, sem))
            at += size
    at = 0
    for (rows, _), out in zip(groups, outs):
        size = depth_of(rows)
        for _ in rows:
            copies.pop(0).wait()
        out[...] = left[at : at + size].T
        at += size


def arrange(place, operand, groups):
    anywhere = pl.BlockSpec(memory_space=pl.ANY)
    depth = sum(depth_of(rows) for rows, _ in groups)
    return pl.pallas_call(
        functools.partial(arrange_kernel, groups),
        out_shape=[
            jax.ShapeDtypeStruct((FEATURES, depth_of(rows)), jnp.bfloat16) for rows, _ in groups
        ],
        in_specs=[pl.BlockSpec(memory_space=pltpu.SMEM), anywhere, anywhere],
        out_specs=[pl.BlockSpec(memory_space=pltpu.VMEM)] * len(groups),
        scratch_shapes=[
            pltpu.VMEM((depth, FEATURES), jnp.bfloat16),
            pltpu.SemaphoreType.DMA((sum(len(rows) for rows, _ in groups),)),
        ],
        compiler_params=pltpu.CompilerParams(vmem_limit_bytes=16 << 20),
        cost_estimate=pl.CostEstimate(flops=0, bytes_accessed=12 << 20, transcendentals=0),
    )(place, *operand)


def contract(left, grads, total=None, dtype=jnp.float32):
    part = jnp.dot(left, jnp.concatenate(grads), preferred_element_type=jnp.float32)
    if total is not None:
        part += total
    return part.astype(dtype)


def depth_of(rows):
    return sum(row[3] for row in rows)


def whole(dzs, dx):
    return [(dz, dx, 0, BLOCK) for dz in dzs]


def parts(rows):
    half, first, second = depth_of(rows) // 2, [], []
    for dz, dx, start, size in rows:
        here = min(size, half)
        if here:
            first.append((dz, dx, start, here))
        if here < size:
            second.append((dz, dx, start + here, size - here))
        half -= here
    return first, second


def body(normed_input, attended, qkv_grad, proj_grad):
    together = lax.optimization_barrier
    row, col = lax.axis_index("row"), lax.axis_index("col")
    place = jnp.stack([row // X, row % X, col // C, col % C])

    tall, wide = qkv_grad, proj_grad
    mine = jnp.concatenate([normed_input, attended], axis=1)

    below, above = hop(tall, 1, 0), hop(tall, -1, 0)
    left, right, opposite = hop(wide, 0, 1), hop(wide, 0, -1), hop(wide, 0, 2)
    down = hop_y(mine, 1)
    below, above, left, right = together((below, above, left, right))
    near = jnp.concatenate([tall, below, above])
    near, opposite = together((near, opposite))
    below, above = hop(below, 1, 0), hop(above, -1, 0)
    near_left, near_right = hop(near, 0, 1), hop(near, 0, -1)
    below, above, opposite, mine, down = together((below, above, opposite, mine, down))
    far = [below, above]
    below, above = hop(below, 1, 0), hop(above, -1, 0)
    far = jnp.concatenate([*far, below, above])
    up = hop_y(mine, -1)
    below, above, far = together((below, above, far))
    mine, up, near_left, near_right = together((mine, up, near_left, near_right))
    across = hop_y(mine, 2)
    far = [far, hop(halves(below)[0], 1, 0), hop(halves(above)[1], -1, 0)]
    wide = jnp.concatenate([wide, left, right, opposite])
    far, wide = together((far, wide))
    far = jnp.concatenate(far)
    far, near_left, near_right = together((far, near_left, near_right))
    far_left, far_right = hop(far, 0, 1), hop(far, 0, -1)
    below, above = hop(wide, 1, 0), hop(wide, -1, 0)
    wide_first = [wide, below, above]
    tall_first = [near, near_left, near_right, far]
    mine = jnp.concatenate([mine, down, up, across])

    near_rows = {dx: whole(NEAR, dx) for dx in X_ORDER}
    far_rows = {dx: whole(FAR, dx) for dx in X_ORDER}
    near_split, far_split = parts(near_rows[2]), parts(far_rows[2])
    wide_rows = {dz: [(dz, dx, 0, BLOCK) for dx in X_ORDER] for dz in range(-4, 5)}
    wide_split = parts(wide_rows[4])
    groups = [
        (near_rows[0] + near_rows[-1] + near_rows[1] + far_rows[0], 0),
        (far_rows[-1] + far_rows[1], 0),
        (near_split[0] + far_split[0] + near_split[1] + far_split[1], 0),
        (wide_rows[0] + wide_rows[-1] + wide_rows[1], 1),
        (sum([wide_rows[d] for d in (-2, 2, -3, 3)], []), 1),
        (wide_split[0] + wide_split[1], 1),
    ]
    lefts = arrange(place, (mine, hop_y(mine, 0, 1)), groups)
    tall_sum = contract(lefts[0], tall_first)

    below, above = hop(below, 1, 0), hop(above, -1, 0)
    wide_second = [below, above]
    wide_sum = contract(lefts[3], wide_first)
    below, above, far_left, far_right = together((below, above, far_left, far_right))
    below, above = hop(below, 1, 0), hop(above, -1, 0)
    first = jnp.concatenate([halves(near_left)[0], halves(far_left)[0]])
    second = jnp.concatenate([halves(near_right)[1], halves(far_right)[1]])
    tall_halves = [hop(first, 0, 1), hop(second, 0, -1)]
    below, above, wide_sum, tall_sum = together((below, above, wide_sum, tall_sum))
    wide_halves = [hop(halves(below)[0], 1, 0), hop(halves(above)[1], -1, 0)]
    tall_sum = contract(lefts[1], [far_left, far_right], tall_sum)
    wide_sum = contract(lefts[4], [*wide_second, below, above], wide_sum)
    tall_sum, wide_sum = together((tall_sum, wide_sum))
    qkv = contract(lefts[2], tall_halves, tall_sum, dtype=jnp.bfloat16)
    out = contract(lefts[5], wide_halves, wide_sum, dtype=jnp.bfloat16)
    return qkv, out


def solution(mesh):
    placed = (P("col", "row"), P("col", "row"), P("row", "col"), P("row", "col"))
    return jax.shard_map(
        body,
        mesh=mesh,
        in_specs=placed,
        out_specs=(P("row", "col"), P("row", "col")),
        check_vma=False,
    )
```

```python
import functools

import jax
import jax.numpy as jnp
from jax import lax
from jax.experimental import pallas as pl
from jax.experimental.pallas import tpu as pltpu
from jax.sharding import PartitionSpec as P

Z, X, Y, C = 8, 4, 4, 2
BLOCK = 64
FEATURES = 512

X_ORDER = (0, -1, 1, 2)
NEAR, FAR = (0, -1, 1), (-2, 2, -3, 3, 4)


def hop(value, dz, dx):
    pairs = [
        (z * X + x, ((z + dz) % Z) * X + (x + dx) % X) for z in range(Z) for x in range(X)
    ]
    return lax.ppermute(value, "row", pairs)


def hop_y(value, dy, swap=0):
    pairs = [(y * C + c, ((y + dy) % Y) * C + (c ^ swap)) for y in range(Y) for c in range(C)]
    return lax.ppermute(value, "col", pairs)


def halves(value):
    half = value.shape[0] // 2
    return value[:half], value[half:]


def arrange_kernel(groups, place_ref, mine_ref, other_ref, *refs):
    outs, (left, sems) = refs[: len(groups)], refs[len(groups) :]
    z, x, y, core = (place_ref[i] for i in range(4))
    at, copies = 0, []
    for rows, op in groups:
        for dz, dx, start, size in rows:
            group = lax.rem(z + (dz + Z), Z)
            away = lax.rem(group // C + Y - y, Y)
            slot = jnp.where(away == 0, 0, jnp.where(away == Y - 1, 1, jnp.where(away == 1, 2, 3)))
            row = slot * (X * BLOCK) + lax.rem(x + (dx + X), X) * BLOCK + start
            source = (pl.ds(pl.multiple_of(row, 32), size), pl.ds(op * FEATURES, FEATURES))
            target = left.at[pl.ds(at, size)]
            swapped, sem = lax.rem(group, C) != core, sems.at[len(copies)]

            @pl.when(swapped)
            def _():
                pltpu.make_async_copy(other_ref.at[source], target, sem).start()

            @pl.when(jnp.logical_not(swapped))
            def _():
                pltpu.make_async_copy(mine_ref.at[source], target, sem).start()

            copies.append(pltpu.make_async_copy(target, target, sem))
            at += size
    at = 0
    for (rows, _), out in zip(groups, outs):
        size = depth_of(rows)
        for _ in rows:
            copies.pop(0).wait()
        out[...] = left[at : at + size].T
        at += size


def arrange(place, operand, groups):
    anywhere = pl.BlockSpec(memory_space=pl.ANY)
    depth = sum(depth_of(rows) for rows, _ in groups)
    return pl.pallas_call(
        functools.partial(arrange_kernel, groups),
        out_shape=[
            jax.ShapeDtypeStruct((FEATURES, depth_of(rows)), jnp.bfloat16) for rows, _ in groups
        ],
        in_specs=[pl.BlockSpec(memory_space=pltpu.SMEM), anywhere, anywhere],
        out_specs=[pl.BlockSpec(memory_space=pltpu.VMEM)] * len(groups),
        scratch_shapes=[
            pltpu.VMEM((depth, FEATURES), jnp.bfloat16),
            pltpu.SemaphoreType.DMA((sum(len(rows) for rows, _ in groups),)),
        ],
        compiler_params=pltpu.CompilerParams(vmem_limit_bytes=16 << 20),
        cost_estimate=pl.CostEstimate(flops=0, bytes_accessed=12 << 20, transcendentals=0),
    )(place, *operand)


def contract(left, grads, total=None, dtype=jnp.float32):
    part = jnp.dot(left, jnp.concatenate(grads), preferred_element_type=jnp.float32)
    if total is not None:
        part += total
    return part.astype(dtype)


def depth_of(rows):
    return sum(row[3] for row in rows)


def whole(dzs, dx):
    return [(dz, dx, 0, BLOCK) for dz in dzs]


def parts(rows):
    half, first, second = depth_of(rows) // 2, [], []
    for dz, dx, start, size in rows:
        here = min(size, half)
        if here:
            first.append((dz, dx, start, here))
        if here < size:
            second.append((dz, dx, start + here, size - here))
        half -= here
    return first, second


def body(normed_input, attended, qkv_grad, proj_grad):
    together = lax.optimization_barrier
    row, col = lax.axis_index("row"), lax.axis_index("col")
    place = jnp.stack([row // X, row % X, col // C, col % C])

    tall, wide = qkv_grad, proj_grad
    mine = jnp.concatenate([normed_input, attended], axis=1)

    below, above = hop(tall, 1, 0), hop(tall, -1, 0)
    left, right, opposite = hop(wide, 0, 1), hop(wide, 0, -1), hop(wide, 0, 2)
    below, above, left, right = together((below, above, left, right))
    near = jnp.concatenate([tall, below, above])
    below, above = hop(below, 1, 0), hop(above, -1, 0)
    near_left, near_right = hop(near, 0, 1), hop(near, 0, -1)
    down = hop_y(mine, 1)
    below, above, opposite = together((below, above, opposite))
    far = [below, above]
    below, above = hop(below, 1, 0), hop(above, -1, 0)
    far = jnp.concatenate([*far, below, above])
    up = hop_y(mine, -1)
    below, above, far = together((below, above, far))
    mine, up, near_left, near_right = together((mine, up, near_left, near_right))
    across = hop_y(mine, 2)
    far = [far, hop(halves(below)[0], 1, 0), hop(halves(above)[1], -1, 0)]
    wide = jnp.concatenate([wide, left, right, opposite])
    far = jnp.concatenate(far)
    far, mine, up = together((far, mine, up))
    far_left, far_right = hop(far, 0, 1), hop(far, 0, -1)
    below, above = hop(wide, 1, 0), hop(wide, -1, 0)
    wide_first = [wide, below, above]
    tall_first = [near, near_left, near_right, far]
    mine = jnp.concatenate([mine, down, up, across])

    near_rows = {dx: whole(NEAR, dx) for dx in X_ORDER}
    far_rows = {dx: whole(FAR, dx) for dx in X_ORDER}
    near_split, far_split = parts(near_rows[2]), parts(far_rows[2])
    wide_rows = {dz: [(dz, dx, 0, BLOCK) for dx in X_ORDER] for dz in range(-4, 5)}
    wide_split = parts(wide_rows[4])
    groups = [
        (near_rows[0] + near_rows[-1] + near_rows[1] + far_rows[0], 0),
        (far_rows[-1] + far_rows[1], 0),
        (near_split[0] + far_split[0] + near_split[1] + far_split[1], 0),
        (wide_rows[0] + wide_rows[-1] + wide_rows[1], 1),
        (sum([wide_rows[d] for d in (-2, 2, -3, 3)], []), 1),
        (wide_split[0] + wide_split[1], 1),
    ]
    lefts = arrange(place, (mine, hop_y(mine, 0, 1)), groups)
    tall_sum = contract(lefts[0], tall_first)

    below, above = hop(below, 1, 0), hop(above, -1, 0)
    wide_second = [below, above]
    wide_sum = contract(lefts[3], wide_first)
    below, above, far_left, far_right = together((below, above, far_left, far_right))
    below, above = hop(below, 1, 0), hop(above, -1, 0)
    first = jnp.concatenate([halves(near_left)[0], halves(far_left)[0]])
    second = jnp.concatenate([halves(near_right)[1], halves(far_right)[1]])

    tall_halves = [hop(first, 0, 1), hop(second, 0, -1)]
    below, above, wide_sum, tall_sum = together((below, above, wide_sum, tall_sum))
    wide_halves = [hop(halves(below)[0], 1, 0), hop(halves(above)[1], -1, 0)]
    tall_sum = contract(lefts[1], [far_left, far_right], tall_sum)
    wide_sum = contract(lefts[4], [*wide_second, below, above], wide_sum)
    tall_sum, wide_sum = together((tall_sum, wide_sum))
    qkv = contract(lefts[2], tall_halves, tall_sum, dtype=jnp.bfloat16)
    out = contract(lefts[5], wide_halves, wide_sum, dtype=jnp.bfloat16)
    return qkv, out


def solution(mesh):
    placed = (P("col", "row"), P("col", "row"), P("row", "col"), P("row", "col"))
    return jax.shard_map(
        body,
        mesh=mesh,
        in_specs=placed,
        out_specs=(P("row", "col"), P("row", "col")),
        check_vma=False,
    )
```

```python
import functools

import jax
import jax.numpy as jnp
from jax import lax
from jax.experimental import pallas as pl
from jax.experimental.pallas import tpu as pltpu
from jax.sharding import PartitionSpec as P

Z, X, Y, C = 8, 4, 4, 2
BLOCK = 64
FEATURES = 512

X_ORDER = (0, -1, 1, 2)
NEAR, FAR = (0, -1, 1), (-2, 2, -3, 3, 4)


def hop(value, dz, dx):
    pairs = [
        (z * X + x, ((z + dz) % Z) * X + (x + dx) % X) for z in range(Z) for x in range(X)
    ]
    return lax.ppermute(value, "row", pairs)


def hop_y(value, dy, swap=0):
    pairs = [(y * C + c, ((y + dy) % Y) * C + (c ^ swap)) for y in range(Y) for c in range(C)]
    return lax.ppermute(value, "col", pairs)


def halves(value):
    half = value.shape[0] // 2
    return value[:half], value[half:]


def arrange_kernel(groups, place_ref, mine_ref, other_ref, *refs):
    outs, (left, sems) = refs[: len(groups)], refs[len(groups) :]
    z, x, y, core = (place_ref[i] for i in range(4))
    at, copies = 0, []
    for rows, op in groups:
        for dz, dx, start, size in rows:
            group = lax.rem(z + (dz + Z), Z)
            away = lax.rem(group // C + Y - y, Y)
            slot = jnp.where(away == 0, 0, jnp.where(away == Y - 1, 1, jnp.where(away == 1, 2, 3)))
            row = slot * (X * BLOCK) + lax.rem(x + (dx + X), X) * BLOCK + start
            source = (pl.ds(pl.multiple_of(row, 32), size), pl.ds(op * FEATURES, FEATURES))
            target = left.at[pl.ds(at, size)]
            swapped, sem = lax.rem(group, C) != core, sems.at[len(copies)]

            @pl.when(swapped)
            def _():
                pltpu.make_async_copy(other_ref.at[source], target, sem).start()

            @pl.when(jnp.logical_not(swapped))
            def _():
                pltpu.make_async_copy(mine_ref.at[source], target, sem).start()

            copies.append(pltpu.make_async_copy(target, target, sem))
            at += size
    at = 0
    for (rows, _), out in zip(groups, outs):
        size = depth_of(rows)
        for _ in rows:
            copies.pop(0).wait()
        out[...] = left[at : at + size].T
        at += size


def arrange(place, operand, groups):
    anywhere = pl.BlockSpec(memory_space=pl.ANY)
    depth = sum(depth_of(rows) for rows, _ in groups)
    return pl.pallas_call(
        functools.partial(arrange_kernel, groups),
        out_shape=[
            jax.ShapeDtypeStruct((FEATURES, depth_of(rows)), jnp.bfloat16) for rows, _ in groups
        ],
        in_specs=[pl.BlockSpec(memory_space=pltpu.SMEM), anywhere, anywhere],
        out_specs=[pl.BlockSpec(memory_space=pltpu.VMEM)] * len(groups),
        scratch_shapes=[
            pltpu.VMEM((depth, FEATURES), jnp.bfloat16),
            pltpu.SemaphoreType.DMA((sum(len(rows) for rows, _ in groups),)),
        ],
        compiler_params=pltpu.CompilerParams(vmem_limit_bytes=16 << 20),
        cost_estimate=pl.CostEstimate(flops=0, bytes_accessed=12 << 20, transcendentals=0),
    )(place, *operand)


def contract(left, grads, total=None, dtype=jnp.float32):
    part = jnp.dot(left, jnp.concatenate(grads), preferred_element_type=jnp.float32)
    if total is not None:
        part += total
    return part.astype(dtype)


def depth_of(rows):
    return sum(row[3] for row in rows)


def whole(dzs, dx):
    return [(dz, dx, 0, BLOCK) for dz in dzs]


def parts(rows):
    half, first, second = depth_of(rows) // 2, [], []
    for dz, dx, start, size in rows:
        here = min(size, half)
        if here:
            first.append((dz, dx, start, here))
        if here < size:
            second.append((dz, dx, start + here, size - here))
        half -= here
    return first, second


def body(normed_input, attended, qkv_grad, proj_grad):
    together = lax.optimization_barrier
    row, col = lax.axis_index("row"), lax.axis_index("col")
    place = jnp.stack([row // X, row % X, col // C, col % C])

    tall, wide = qkv_grad, proj_grad
    mine = jnp.concatenate([normed_input, attended], axis=1)

    below, above = hop(tall, 1, 0), hop(tall, -1, 0)
    left, right, opposite = hop(wide, 0, 1), hop(wide, 0, -1), hop(wide, 0, 2)
    below, above, left, right = together((below, above, left, right))
    near = jnp.concatenate([tall, below, above])
    near, opposite = together((near, opposite))
    below, above = hop(below, 1, 0), hop(above, -1, 0)
    near_left, near_right = hop(near, 0, 1), hop(near, 0, -1)
    down = hop_y(mine, 1)
    below, above, left, right, opposite, mine, down = together((below, above, left, right, opposite, mine, down))
    far = [below, above]
    below, above = hop(below, 1, 0), hop(above, -1, 0)
    far = jnp.concatenate([*far, below, above])
    up = hop_y(mine, -1)
    below, above, far = together((below, above, far))
    mine, up, near_left, near_right = together((mine, up, near_left, near_right))
    across = hop_y(mine, 2)
    far = [far, hop(halves(below)[0], 1, 0), hop(halves(above)[1], -1, 0)]
    wide = jnp.concatenate([wide, left, right, opposite])
    far = jnp.concatenate(far)
    far, mine, up = together((far, mine, up))
    far_left, far_right = hop(far, 0, 1), hop(far, 0, -1)
    below, above = hop(wide, 1, 0), hop(wide, -1, 0)
    wide_first = [wide, below, above]
    tall_first = [near, near_left, near_right, far]
    mine = jnp.concatenate([mine, down, up, across])

    near_rows = {dx: whole(NEAR, dx) for dx in X_ORDER}
    far_rows = {dx: whole(FAR, dx) for dx in X_ORDER}
    near_split, far_split = parts(near_rows[2]), parts(far_rows[2])
    wide_rows = {dz: [(dz, dx, 0, BLOCK) for dx in X_ORDER] for dz in range(-4, 5)}
    wide_split = parts(wide_rows[4])
    groups = [
        (near_rows[0] + near_rows[-1] + near_rows[1] + far_rows[0], 0),
        (far_rows[-1] + far_rows[1], 0),
        (near_split[0] + far_split[0] + near_split[1] + far_split[1], 0),
        (wide_rows[0] + wide_rows[-1] + wide_rows[1], 1),
        (sum([wide_rows[d] for d in (-2, 2, -3, 3)], []), 1),
        (wide_split[0] + wide_split[1], 1),
    ]
    lefts = arrange(place, (mine, hop_y(mine, 0, 1)), groups)
    tall_sum = contract(lefts[0], tall_first)

    below, above = hop(below, 1, 0), hop(above, -1, 0)
    wide_second = [below, above]
    wide_sum = contract(lefts[3], wide_first)
    below, above, far_left, far_right = together((below, above, far_left, far_right))
    below, above = hop(below, 1, 0), hop(above, -1, 0)
    first = jnp.concatenate([halves(near_left)[0], halves(far_left)[0]])
    second = jnp.concatenate([halves(near_right)[1], halves(far_right)[1]])

    tall_halves = [hop(first, 0, 1), hop(second, 0, -1)]
    below, above, wide_sum, tall_sum = together((below, above, wide_sum, tall_sum))
    wide_halves = [hop(halves(below)[0], 1, 0), hop(halves(above)[1], -1, 0)]
    tall_sum = contract(lefts[1], [far_left, far_right], tall_sum)
    wide_sum = contract(lefts[4], [*wide_second, below, above], wide_sum)
    tall_sum, wide_sum = together((tall_sum, wide_sum))
    qkv = contract(lefts[2], tall_halves, tall_sum, dtype=jnp.bfloat16)
    out = contract(lefts[5], wide_halves, wide_sum, dtype=jnp.bfloat16)
    return qkv, out


def solution(mesh):
    placed = (P("col", "row"), P("col", "row"), P("row", "col"), P("row", "col"))
    return jax.shard_map(
        body,
        mesh=mesh,
        in_specs=placed,
        out_specs=(P("row", "col"), P("row", "col")),
        check_vma=False,
    )
```

```python
import functools

import jax
import jax.numpy as jnp
from jax import lax
from jax.experimental import pallas as pl
from jax.experimental.pallas import tpu as pltpu
from jax.sharding import PartitionSpec as P

Z, X, Y, C = 8, 4, 4, 2
BLOCK = 64
FEATURES = 512

X_ORDER = (0, -1, 1, 2)
NEAR, FAR = (0, -1, 1), (-2, 2, -3, 3, 4)


def hop(value, dz, dx):
    pairs = [
        (z * X + x, ((z + dz) % Z) * X + (x + dx) % X) for z in range(Z) for x in range(X)
    ]
    return lax.ppermute(value, "row", pairs)


def hop_y(value, dy, swap=0):
    pairs = [(y * C + c, ((y + dy) % Y) * C + (c ^ swap)) for y in range(Y) for c in range(C)]
    return lax.ppermute(value, "col", pairs)


def halves(value):
    half = value.shape[0] // 2
    return value[:half], value[half:]


def arrange_kernel(groups, place_ref, mine_ref, other_ref, *refs):
    outs, (left, sems) = refs[: len(groups)], refs[len(groups) :]
    z, x, y, core = (place_ref[i] for i in range(4))
    at, copies = 0, []
    for rows, op in groups:
        for dz, dx, start, size in rows:
            group = lax.rem(z + (dz + Z), Z)
            away = lax.rem(group // C + Y - y, Y)
            slot = jnp.where(away == 0, 0, jnp.where(away == Y - 1, 1, jnp.where(away == 1, 2, 3)))
            row = slot * (X * BLOCK) + lax.rem(x + (dx + X), X) * BLOCK + start
            source = (pl.ds(pl.multiple_of(row, 32), size), pl.ds(op * FEATURES, FEATURES))
            target = left.at[pl.ds(at, size)]
            swapped, sem = lax.rem(group, C) != core, sems.at[len(copies)]

            @pl.when(swapped)
            def _():
                pltpu.make_async_copy(other_ref.at[source], target, sem).start()

            @pl.when(jnp.logical_not(swapped))
            def _():
                pltpu.make_async_copy(mine_ref.at[source], target, sem).start()

            copies.append(pltpu.make_async_copy(target, target, sem))
            at += size
    at = 0
    for (rows, _), out in zip(groups, outs):
        size = depth_of(rows)
        for _ in rows:
            copies.pop(0).wait()
        out[...] = left[at : at + size].T
        at += size


def arrange(place, operand, groups):
    anywhere = pl.BlockSpec(memory_space=pl.ANY)
    depth = sum(depth_of(rows) for rows, _ in groups)
    return pl.pallas_call(
        functools.partial(arrange_kernel, groups),
        out_shape=[
            jax.ShapeDtypeStruct((FEATURES, depth_of(rows)), jnp.bfloat16) for rows, _ in groups
        ],
        in_specs=[pl.BlockSpec(memory_space=pltpu.SMEM), anywhere, anywhere],
        out_specs=[pl.BlockSpec(memory_space=pltpu.VMEM)] * len(groups),
        scratch_shapes=[
            pltpu.VMEM((depth, FEATURES), jnp.bfloat16),
            pltpu.SemaphoreType.DMA((sum(len(rows) for rows, _ in groups),)),
        ],
        compiler_params=pltpu.CompilerParams(vmem_limit_bytes=16 << 20),
        cost_estimate=pl.CostEstimate(flops=0, bytes_accessed=12 << 20, transcendentals=0),
    )(place, *operand)


def contract(left, grads, total=None, dtype=jnp.float32):
    part = jnp.dot(left, jnp.concatenate(grads), preferred_element_type=jnp.float32)
    if total is not None:
        part += total
    return part.astype(dtype)


def depth_of(rows):
    return sum(row[3] for row in rows)


def whole(dzs, dx):
    return [(dz, dx, 0, BLOCK) for dz in dzs]


def parts(rows):
    half, first, second = depth_of(rows) // 2, [], []
    for dz, dx, start, size in rows:
        here = min(size, half)
        if here:
            first.append((dz, dx, start, here))
        if here < size:
            second.append((dz, dx, start + here, size - here))
        half -= here
    return first, second


def body(normed_input, attended, qkv_grad, proj_grad):
    together = lax.optimization_barrier
    row, col = lax.axis_index("row"), lax.axis_index("col")
    place = jnp.stack([row // X, row % X, col // C, col % C])

    tall, wide = qkv_grad, proj_grad
    mine = jnp.concatenate([normed_input, attended], axis=1)

    below, above = hop(tall, 1, 0), hop(tall, -1, 0)
    left, right, opposite = hop(wide, 0, 1), hop(wide, 0, -1), hop(wide, 0, 2)
    below, above, left, right = together((below, above, left, right))
    near = jnp.concatenate([tall, below, above])
    near, opposite = together((near, opposite))
    below, above = hop(below, 1, 0), hop(above, -1, 0)
    near_left, near_right = hop(near, 0, 1), hop(near, 0, -1)
    down = hop_y(mine, 1)
    below, above, left, right, opposite, mine, down = together((below, above, left, right, opposite, mine, down))
    far = [below, above]
    below, above = hop(below, 1, 0), hop(above, -1, 0)
    far = jnp.concatenate([*far, below, above])
    up = hop_y(mine, -1)
    below, above, far = together((below, above, far))
    mine, up, near_left, near_right = together((mine, up, near_left, near_right))
    across = hop_y(mine, 2)
    far = [far, hop(halves(below)[0], 1, 0), hop(halves(above)[1], -1, 0)]
    wide = jnp.concatenate([wide, left, right, opposite])
    far = jnp.concatenate(far)
    far, mine, up = together((far, mine, up))
    far_left, far_right = hop(far, 0, 1), hop(far, 0, -1)
    below, above = hop(wide, 1, 0), hop(wide, -1, 0)
    wide_first = [wide, below, above]
    tall_first = [near, near_left, near_right, far]
    mine = jnp.concatenate([mine, down, up, across])

    near_rows = {dx: whole(NEAR, dx) for dx in X_ORDER}
    far_rows = {dx: whole(FAR, dx) for dx in X_ORDER}
    near_split, far_split = parts(near_rows[2]), parts(far_rows[2])
    wide_rows = {dz: [(dz, dx, 0, BLOCK) for dx in X_ORDER] for dz in range(-4, 5)}
    wide_split = parts(wide_rows[4])
    groups = [
        (near_rows[0] + near_rows[-1] + near_rows[1] + far_rows[0], 0),
        (far_rows[-1] + far_rows[1], 0),
        (near_split[0] + far_split[0] + near_split[1] + far_split[1], 0),
        (wide_rows[0] + wide_rows[-1] + wide_rows[1], 1),
        (sum([wide_rows[d] for d in (-2, 2, -3, 3)], []), 1),
        (wide_split[0] + wide_split[1], 1),
    ]
    lefts = arrange(place, (mine, hop_y(mine, 0, 1)), groups)
    tall_sum = contract(lefts[0], tall_first)

    below, above = hop(below, 1, 0), hop(above, -1, 0)
    wide_second = [below, above]
    wide_sum = contract(lefts[3], wide_first)
    below, above, far_left, far_right = together((below, above, far_left, far_right))
    below, above = hop(below, 1, 0), hop(above, -1, 0)
    first = jnp.concatenate([halves(near_left)[0], halves(far_left)[0]])
    second = jnp.concatenate([halves(near_right)[1], halves(far_right)[1]])

    tall_halves = [hop(first, 0, 1), hop(second, 0, -1)]
    tall_sum = contract(lefts[1], [far_left, far_right], tall_sum)
    below, above, wide_sum, tall_sum = together((below, above, wide_sum, tall_sum))
    wide_halves = [hop(halves(below)[0], 1, 0), hop(halves(above)[1], -1, 0)]
    wide_sum = contract(lefts[4], [*wide_second, below, above], wide_sum)
    tall_halves, wide_sum = together((tall_halves, wide_sum))
    qkv = contract(lefts[2], tall_halves, tall_sum, dtype=jnp.bfloat16)
    out = contract(lefts[5], wide_halves, wide_sum, dtype=jnp.bfloat16)
    return qkv, out


def solution(mesh):
    placed = (P("col", "row"), P("col", "row"), P("row", "col"), P("row", "col"))
    return jax.shard_map(
        body,
        mesh=mesh,
        in_specs=placed,
        out_specs=(P("row", "col"), P("row", "col")),
        check_vma=False,
    )
```

```python
import functools

import jax
import jax.numpy as jnp
from jax import lax
from jax.experimental import pallas as pl
from jax.experimental.pallas import tpu as pltpu
from jax.sharding import PartitionSpec as P

Z, X, Y, C = 8, 4, 4, 2
BLOCK = 64
FEATURES = 512

X_ORDER = (0, -1, 1, 2)
NEAR, FAR = (0, -1, 1), (-2, 2, -3, 3, 4)


def hop(value, dz, dx):
    pairs = [
        (z * X + x, ((z + dz) % Z) * X + (x + dx) % X) for z in range(Z) for x in range(X)
    ]
    return lax.ppermute(value, "row", pairs)


def hop_y(value, dy, swap=0):
    pairs = [(y * C + c, ((y + dy) % Y) * C + (c ^ swap)) for y in range(Y) for c in range(C)]
    return lax.ppermute(value, "col", pairs)


def halves(value):
    half = value.shape[0] // 2
    return value[:half], value[half:]


def arrange_kernel(groups, place_ref, mine_ref, other_ref, *refs):
    outs, (left, sems) = refs[: len(groups)], refs[len(groups) :]
    z, x, y, core = (place_ref[i] for i in range(4))
    at, copies = 0, []
    for rows, op in groups:
        for dz, dx, start, size in rows:
            group = lax.rem(z + (dz + Z), Z)
            away = lax.rem(group // C + Y - y, Y)
            slot = jnp.where(away == 0, 0, jnp.where(away == Y - 1, 1, jnp.where(away == 1, 2, 3)))
            row = slot * (X * BLOCK) + lax.rem(x + (dx + X), X) * BLOCK + start
            source = (pl.ds(pl.multiple_of(row, 32), size), pl.ds(op * FEATURES, FEATURES))
            target = left.at[pl.ds(at, size)]
            swapped, sem = lax.rem(group, C) != core, sems.at[len(copies)]

            @pl.when(swapped)
            def _():
                pltpu.make_async_copy(other_ref.at[source], target, sem).start()

            @pl.when(jnp.logical_not(swapped))
            def _():
                pltpu.make_async_copy(mine_ref.at[source], target, sem).start()

            copies.append(pltpu.make_async_copy(target, target, sem))
            at += size
    at = 0
    for (rows, _), out in zip(groups, outs):
        size = depth_of(rows)
        for _ in rows:
            copies.pop(0).wait()
        out[...] = left[at : at + size].T
        at += size


def arrange(place, operand, groups):
    anywhere = pl.BlockSpec(memory_space=pl.ANY)
    depth = sum(depth_of(rows) for rows, _ in groups)
    return pl.pallas_call(
        functools.partial(arrange_kernel, groups),
        out_shape=[
            jax.ShapeDtypeStruct((FEATURES, depth_of(rows)), jnp.bfloat16) for rows, _ in groups
        ],
        in_specs=[pl.BlockSpec(memory_space=pltpu.SMEM), anywhere, anywhere],
        out_specs=[pl.BlockSpec(memory_space=pltpu.VMEM)] * len(groups),
        scratch_shapes=[
            pltpu.VMEM((depth, FEATURES), jnp.bfloat16),
            pltpu.SemaphoreType.DMA((sum(len(rows) for rows, _ in groups),)),
        ],
        compiler_params=pltpu.CompilerParams(vmem_limit_bytes=16 << 20),
        cost_estimate=pl.CostEstimate(flops=0, bytes_accessed=12 << 20, transcendentals=0),
    )(place, *operand)


def contract(left, grads, total=None, dtype=jnp.float32):
    part = jnp.dot(left, jnp.concatenate(grads), preferred_element_type=jnp.float32)
    if total is not None:
        part += total
    return part.astype(dtype)


def depth_of(rows):
    return sum(row[3] for row in rows)


def whole(dzs, dx):
    return [(dz, dx, 0, BLOCK) for dz in dzs]


def parts(rows):
    half, first, second = depth_of(rows) // 2, [], []
    for dz, dx, start, size in rows:
        here = min(size, half)
        if here:
            first.append((dz, dx, start, here))
        if here < size:
            second.append((dz, dx, start + here, size - here))
        half -= here
    return first, second


def body(normed_input, attended, qkv_grad, proj_grad):
    together = lax.optimization_barrier
    row, col = lax.axis_index("row"), lax.axis_index("col")
    place = jnp.stack([row // X, row % X, col // C, col % C])

    tall, wide = qkv_grad, proj_grad
    mine = jnp.concatenate([normed_input, attended], axis=1)

    below, above = hop(tall, 1, 0), hop(tall, -1, 0)
    left, right, opposite = hop(wide, 0, 1), hop(wide, 0, -1), hop(wide, 0, 2)
    below, above, left, right = together((below, above, left, right))
    near = jnp.concatenate([tall, below, above])
    near, opposite = together((near, opposite))
    below, above = hop(below, 1, 0), hop(above, -1, 0)
    near_left, near_right = hop(near, 0, 1), hop(near, 0, -1)
    down = hop_y(mine, 1)
    below, above, left, right, opposite, mine, down = together((below, above, left, right, opposite, mine, down))
    far = [below, above]
    below, above = hop(below, 1, 0), hop(above, -1, 0)
    far = jnp.concatenate([*far, below, above])
    up = hop_y(mine, -1)
    below, above, far = together((below, above, far))
    mine, up, near_left, near_right = together((mine, up, near_left, near_right))
    across = hop_y(mine, 2)
    far = [far, hop(halves(below)[0], 1, 0), hop(halves(above)[1], -1, 0)]
    wide = jnp.concatenate([wide, left, right, opposite])
    far = jnp.concatenate(far)
    far, mine, up = together((far, mine, up))
    far_left, far_right = hop(far, 0, 1), hop(far, 0, -1)
    below, above = hop(wide, 1, 0), hop(wide, -1, 0)
    wide_first = [wide, below, above]
    tall_first = [near, near_left, near_right, far]
    mine = jnp.concatenate([mine, down, up, across])

    near_rows = {dx: whole(NEAR, dx) for dx in X_ORDER}
    far_rows = {dx: whole(FAR, dx) for dx in X_ORDER}
    near_split, far_split = parts(near_rows[2]), parts(far_rows[2])
    wide_rows = {dz: [(dz, dx, 0, BLOCK) for dx in X_ORDER] for dz in range(-4, 5)}
    wide_split = parts(wide_rows[4])
    groups = [
        (sum([near_rows[0], near_rows[-1], near_rows[1], *(far_rows[d] for d in (0, -1, 1))], []), 0),
        (near_split[0] + far_split[0] + near_split[1] + far_split[1], 0),
        (wide_rows[0] + wide_rows[-1] + wide_rows[1], 1),
        (sum([wide_rows[d] for d in (-2, 2, -3, 3)], []), 1),
        (wide_split[0] + wide_split[1], 1),
    ]
    lefts = arrange(place, (mine, hop_y(mine, 0, 1)), groups)

    below, above = hop(below, 1, 0), hop(above, -1, 0)
    wide_second = [below, above]
    wide_sum = contract(lefts[2], wide_first)
    tall_sum = contract(lefts[0], [*tall_first, far_left, far_right])
    below, above, far_left, far_right = together((below, above, far_left, far_right))
    below, above = hop(below, 1, 0), hop(above, -1, 0)
    first = jnp.concatenate([halves(near_left)[0], halves(far_left)[0]])
    second = jnp.concatenate([halves(near_right)[1], halves(far_right)[1]])

    tall_halves = [hop(first, 0, 1), hop(second, 0, -1)]
    below, above, wide_sum, tall_sum = together((below, above, wide_sum, tall_sum))
    wide_halves = [hop(halves(below)[0], 1, 0), hop(halves(above)[1], -1, 0)]
    wide_sum = contract(lefts[3], [*wide_second, below, above], wide_sum)
    tall_halves, wide_sum = together((tall_halves, wide_sum))
    qkv = contract(lefts[1], tall_halves, tall_sum, dtype=jnp.bfloat16)
    out = contract(lefts[4], wide_halves, wide_sum, dtype=jnp.bfloat16)
    return qkv, out


def solution(mesh):
    placed = (P("col", "row"), P("col", "row"), P("row", "col"), P("row", "col"))
    return jax.shard_map(
        body,
        mesh=mesh,
        in_specs=placed,
        out_specs=(P("row", "col"), P("row", "col")),
        check_vma=False,
    )
```
